32 devices in a mesh: section: 2 (over core), seq: 4 (over z), head: 4 (over y, x).
Axes of the slice: x: 2, y: 2, z: 4, core: 2. Of those that a mesh axis runs over, the one named last changes fastest.
Arguments:
- inputs: bfloat16 [2, 512, 1024], P(None, 'seq'), may hold values from -6 to 6
- cotangent: bfloat16 [2, 512, 1024], P(None, 'seq'), may hold values from -6 to 6
- gains: float32 [2, 2, 1024], P('section'), may hold values from 0.5 to 1.5
- w_in: bfloat16 [2, 1024, 8, 768], P('section', None, 'head'), may hold values from -0.1875 to 0.1875
- w_rates: bfloat16 [2, 2, 1024, 8], P('section', None, None, 'head'), may hold values from -0.1875 to 0.1875
- a_log: float32 [2, 8], P('section', 'head'), may hold values from -3 to 1
- dt_bias: float32 [2, 8], P('section', 'head'), may hold values from -7 to -2.3
- conv_kernel: float32 [2, 4, 8, 512], P('section', None, 'head'), may hold values from -3 to 3
- out_gain: float32 [2, 256], P('section'), may hold values from 0.5 to 1.5
- w_out: bfloat16 [2, 8, 256, 1024], P('section', 'head'), may hold values from -0.25 to 0.25
- w_ffn_in: bfloat16 [2, 1024, 2, 2816], P('section', None, None, 'head'), may hold values from -0.1875 to 0.1875
- w_down: bfloat16 [2, 2816, 1024], P('section', 'head'), may hold values from -0.21875 to 0.21875
Outputs:
- block_out: bfloat16 [2, 2, 512, 1024], P('section', None, 'seq')
- input_grad: bfloat16 [2, 2, 512, 1024], P('section', None, 'seq')
- gains_grad: float32 [2, 2, 1024], P('section')
- w_in_grad: float32 [2, 1024, 8, 768], P('section', 'seq', 'head')
- w_rates_grad: float32 [2, 2, 1024, 8], P('section', None, 'seq', 'head')
- a_log_grad: float32 [2, 8], P('section', 'head')
- dt_bias_grad: float32 [2, 8], P('section', 'head')
- conv_grad: float32 [2, 4, 8, 512], P('section', None, 'head')
- out_gain_grad: float32 [2, 256], P('section')
- w_out_grad: float32 [2, 8, 256, 1024], P('section', 'head', None, 'seq')
- w_ffn_in_grad: float32 [2, 1024, 2, 2816], P('section', 'seq', None, 'head')
- w_down_grad: float32 [2, 2816, 1024], P('section', 'head', 'seq')
The draws below stay inside these ranges and needn't reach their ends.
All inputs are finite; a program needn't handle non-finite values.
Results may differ from the reference program's by a relative error of at most 0.035.
Values may be sent and summed in bfloat16 or wider, within the bound.
No kernel may reach another device: no remote copies, remote signals or barrier semaphores. Data moves between devices by JAX's collectives and lax.ppermute only.
A program may use at most 192 MiB of HBM per device.

```python
import jax
import jax.numpy as jnp
from jax import lax

D = 1024
HEADS = 8
DK = 128
DV = 256
FF = 2816
KW = 4
GROUP = 64
MB = 2
L = 512
QKV = 512
PROJ = 768


def levels(stream_key, shape, cuts, smallest, top_value):
    def one(position, blocks):
        draws = jax.random.uniform(jax.random.fold_in(jax.random.fold_in(stream_key, 6), position), (blocks,), jnp.float32, smallest / len(cuts), top_value / len(cuts))
        return jnp.repeat(jnp.exp(draws), shape[position] // blocks).reshape((-1,) + (1,) * (len(shape) - position - 1))

    loudness = one(*cuts[0])
    for cut in cuts[1:]:
        loudness = loudness * one(*cut)
    return loudness


def bell_draw(own_key, extent, scale, most, cuts=(), kind=jnp.bfloat16):
    level = levels(own_key, extent, cuts, -0.22, 0.18) if cuts else 1.0
    values = jax.random.normal(own_key, extent, jnp.float32) * scale * level
    return jnp.minimum(jnp.maximum(values, -most), most).astype(kind)


def setup_inputs(seed: int = 0) -> dict:
    splits = jax.random.split(jax.random.key(seed), 13)
    return {
        "inputs": bell_draw(splits[0], (MB, L, D), 1.0, 6.0, ((1, 4),)),
        "cotangent": bell_draw(splits[1], (MB, L, D), 1.0, 6.0, ((1, 4),)),
        "gains": jnp.clip(1.0 + 0.1 * jax.random.normal(splits[2], (2, 2, D), jnp.float32), 0.5, 1.5),
        "w_in": bell_draw(splits[3], (2, D, HEADS, PROJ), D ** -0.5, 0.1875, ((0, 2), (2, 4))),
        "w_rates": bell_draw(splits[4], (2, 2, D, HEADS), D ** -0.5, 0.1875, ((0, 2), (3, 4))),
        "a_log": jnp.clip(-3.0 + 4.0 * jax.random.uniform(splits[5], (2, HEADS), jnp.float32) ** levels(splits[5], (2, HEADS), ((0, 2), (1, 4)), -0.2, 0.2), -3.0, 1.0),
        "dt_bias": jnp.clip(-7.0 + 4.7 * jax.random.uniform(splits[6], (2, HEADS), jnp.float32) ** levels(splits[6], (2, HEADS), ((0, 2), (1, 4)), -0.2, 0.2), -7.0, -2.3),
        "conv_kernel": bell_draw(splits[7], (2, KW, HEADS, QKV), 0.5, 3.0, ((0, 2), (2, 4)), jnp.float32),
        "out_gain": jnp.clip(1.0 + 0.1 * jax.random.normal(splits[8], (2, DV), jnp.float32), 0.5, 1.5),
        "w_out": bell_draw(splits[9], (2, HEADS, DV, D), (HEADS * DV // 4) ** -0.5, 0.25, ((0, 2), (1, 4))),
        "w_ffn_in": bell_draw(splits[10], (2, D, 2, FF), D ** -0.5, 0.1875, ((0, 2), (3, 4))),
        "w_down": bell_draw(splits[11], (2, FF, D), (FF // 4) ** -0.5, 0.21875, ((0, 2), (1, 4))),
    }


@jax.custom_vjp
def low(v):
    return lax.optimization_barrier(v.astype(jnp.bfloat16)).astype(jnp.float32)

@jax.custom_vjp
def low_back(v):
    return v

def low_keep(v):
    return (low(v), None)

def low_pass(kept, grad):
    return (grad,)

def back_keep(v):
    return (v, None)

def back_low(kept, grad):
    return (low(grad),)
low.defvjp(low_keep, low_pass)
low_back.defvjp(back_keep, back_low)
EPSILON = 1e-06
head_epsilon = 0.01
highest_precision = lax.Precision.HIGHEST

def root_norm(values, gain):
    return values * lax.rsqrt(lax.optimization_barrier(jnp.mean(values * values, axis=-1, keepdims=True)) + EPSILON) * gain

def head_norm(values, gain):
    return values * lax.rsqrt(lax.optimization_barrier(jnp.mean(values * values, axis=-1, keepdims=True)) + head_epsilon) * gain

def unit_norm(values):
    return values * lax.rsqrt(lax.optimization_barrier(jnp.sum(values * values, axis=-1, keepdims=True)) + EPSILON)

def prepare(extended, kernel, decay_raw, strength_raw, decay_log, decay_bias):
    kernel_size = kernel.shape[0]
    length = extended.shape[0] - kernel_size + 1
    convolved = kernel[0] * extended[0:length]
    for offset in range(1, kernel_size):
        convolved = convolved + kernel[offset] * extended[offset:offset + length]
    active = jax.nn.silu(convolved)
    query_rows = unit_norm(active[..., :DK]) * DK ** (-0.5)
    key_rows = unit_norm(active[..., DK:2 * DK])
    values = active[..., 2 * DK:]
    strength = jax.nn.sigmoid(strength_raw)
    log_decay = -jnp.exp(decay_log) * jax.nn.softplus(decay_raw + decay_bias)
    return (query_rows, key_rows, values, strength, log_decay)

def split_blocks(array):
    return array.reshape((array.shape[0] // GROUP, GROUP) + array.shape[1:])

def group_core(key_rows, values, strength, log_decay):
    length = log_decay.shape[0]
    running_total = jnp.cumsum(log_decay, axis=0)
    row_ids = lax.broadcasted_iota(jnp.int32, (length, length), 0)
    columns = lax.broadcasted_iota(jnp.int32, (length, length), 1)
    spread = jnp.transpose(running_total)[:, :, None] - jnp.transpose(running_total)[:, None, :]
    within = jnp.where(row_ids >= columns, jnp.exp(jnp.where(row_ids >= columns, spread, 0.0)), 0.0)
    strictly_below = jnp.where(row_ids > columns, within, 0.0)
    weighted = key_rows * strength[..., None]
    lower_matrix = jnp.eye(length, dtype=jnp.float32) + jnp.einsum('ihd,jhd->hij', weighted, key_rows, precision=highest_precision) * strictly_below
    right_values = jnp.transpose(values * strength[..., None], (1, 0, 2))
    right_keys = jnp.transpose(weighted * jnp.exp(running_total)[..., None], (1, 0, 2))
    value_solution = lax.linalg.triangular_solve(lower_matrix, right_values, left_side=True, lower=True)
    key_solution = lax.linalg.triangular_solve(lower_matrix, right_keys, left_side=True, lower=True)
    ending_key_rows = key_rows * jnp.exp(running_total[-1:] - running_total)[..., None]
    return (running_total, within, value_solution, key_solution, ending_key_rows)

def group_advance(current_state, query_rows, key_rows, running_total, within, value_solution, key_solution, ending_key_rows):
    scores = jnp.einsum('ihd,jhd->hij', query_rows, key_rows, precision=highest_precision) * within
    corrected_values = value_solution - jnp.einsum('jwm,jma->jwa', key_solution, current_state, precision=highest_precision)
    output_rows = jnp.einsum('ywj,wji->ywi', query_rows * jnp.exp(running_total)[..., None], current_state, precision=highest_precision)
    output_rows = output_rows + jnp.einsum('hij,hjv->ihv', scores, corrected_values, precision=highest_precision)
    updated_state = jnp.exp(running_total[-1])[:, None, None] * current_state + jnp.einsum('zqy,qzo->qyo', ending_key_rows, corrected_values, precision=highest_precision)
    return (updated_state, output_rows)

def delta_rule(query_rows, key_rows, values, strength, log_decay):

    def one_block(current_state, pieces):
        block_queries, block_keys, value_block_rows, block_strength, block_decay = pieces
        tables = group_core(block_keys, value_block_rows, block_strength, block_decay)
        return group_advance(current_state, block_queries, block_keys, *tables)
    initial = jnp.zeros((query_rows.shape[1], query_rows.shape[2], values.shape[2]), jnp.float32)
    unused, output_rows = lax.scan(jax.checkpoint(one_block), initial, (split_blocks(query_rows), split_blocks(key_rows), split_blocks(values), split_blocks(strength), split_blocks(log_decay)))
    return output_rows.reshape(query_rows.shape[:2] + (values.shape[2],))

def block(stream, weights):
    gains, w_in, w_rates, a_log, dt_bias, conv_kernel, out_gain, w_out, w_ffn_in, w_down = weights
    normed = low(root_norm(stream, gains[0]))
    projected = jnp.einsum('ld,dhp->lhp', normed, w_in, precision=highest_precision)
    mixed_pre = low_back(low(projected[..., :QKV]))
    gate_pre = low_back(projected[..., QKV:])
    rate_logits = low_back(jnp.einsum('ld,rdh->lrh', normed, w_rates, precision=highest_precision))
    extended = jnp.concatenate([jnp.zeros((KW - 1,) + mixed_pre.shape[1:], jnp.float32), mixed_pre], axis=0)
    query_rows, key_rows, values, strength, log_decay = prepare(extended, conv_kernel, rate_logits[:, 0], rate_logits[:, 1], a_log, dt_bias)
    output_rows = delta_rule(low(query_rows), low(key_rows), low(values), strength, log_decay)
    gated = low(head_norm(output_rows, out_gain) * jax.nn.silu(gate_pre))
    mixer_out = low_back(jnp.einsum('lhv,hvd->ld', gated, w_out, precision=highest_precision))
    hidden = stream + mixer_out
    hidden_norm = low(root_norm(hidden, gains[1]))
    gate_up = low_back(jnp.einsum('ld,dgf->lgf', hidden_norm, w_ffn_in, precision=highest_precision))
    active = low(jax.nn.silu(gate_up[:, 0]) * gate_up[:, 1])
    return hidden + low_back(jnp.dot(active, w_down, precision=highest_precision))

def reference(inputs, cotangent, gains, w_in, w_rates, a_log, dt_bias, conv_kernel, out_gain, w_out, w_ffn_in, w_down):
    params = tuple((weight.astype(jnp.float32) for weight in (gains, w_in, w_rates, a_log, dt_bias, conv_kernel, out_gain, w_out, w_ffn_in, w_down)))
    stream = inputs.astype(jnp.float32)
    boundary = jnp.zeros_like(stream)

    def forward(stream, params, boundary):
        first_params = tuple((weight[0] for weight in params))
        second_params = tuple((weight[1] for weight in params))
        first_outs = []
        final_outs = []
        for member in range(MB):
            first_out = low_back(low(block(stream[member], first_params)) + boundary[member])
            final_outs.append(block(first_out, second_params))
            first_outs.append(first_out)
        return (jnp.stack(final_outs), jnp.stack(first_outs))
    final_all, vjp_fn, first_all = jax.vjp(forward, stream, params, boundary, has_aux=True)
    grad_stream, grad_params, grad_boundary = vjp_fn(cotangent.astype(jnp.float32))
    block_out = jnp.stack([first_all, final_all]).astype(jnp.bfloat16)
    input_grad = jnp.stack([grad_stream, grad_boundary]).astype(jnp.bfloat16)
    return (block_out, input_grad, grad_params[0], grad_params[1], grad_params[2], grad_params[3], grad_params[4], grad_params[5], grad_params[6], grad_params[7], grad_params[8], grad_params[9])
```

```python
import functools

import jax
import jax.numpy as jnp
from jax import lax
from jax.experimental import pallas as pl
from jax.experimental.pallas import tpu as pltpu
from jax.sharding import PartitionSpec as P

DK = 128
DV = 256
KW = 4
CHUNK = 128
LANES = 128
EPS = 1e-06
HEAD_EPS = 0.01
AXES = ("section", "seq", "head")
KERNELS = True
F32 = jnp.float32
BF16 = jnp.bfloat16


def route(move):
    sections, seqs, heads = (lax.axis_size(axis) for axis in AXES)
    pairs = []
    for s in range(sections):
        for z in range(seqs):
            for h in range(heads):
                s2, z2, h2 = move(s, z, h)
                pairs.append(((s * seqs + z) * heads + h, (s2 * seqs + z2) * heads + h2))
    return pairs


def swap_section(value):
    return lax.ppermute(value, AXES, route(lambda s, z, h: (1 - s, z, h)))


def sum_heads(part):
    total = part.astype(BF16)
    step = 1
    while step < lax.axis_size("head"):
        other = lax.ppermute(total, AXES, route(lambda s, z, h: (s, z, h ^ step)))
        total = (total.astype(F32) + other.astype(F32)).astype(BF16 if step * 2 < lax.axis_size("head") else F32)
        step *= 2
    return total.astype(F32)


def sum_seq(part):
    total = part
    step = 1
    while step < lax.axis_size("seq"):
        total = total + lax.ppermute(total, AXES, route(lambda s, z, h: (s, z ^ step, h)))
        step *= 2
    return total


def exchange_seq(value):
    return lax.all_to_all(value, "seq", 0, 0, tiled=False)


NN = (((1,), (0,)), ((), ()))
NT = (((1,), (1,)), ((), ()))
TN = (((0,), (0,)), ((), ()))


def raw(a, b, dims, passes):
    a_hi, b_hi = a.astype(BF16), b.astype(BF16)
    out = lax.dot_general(a_hi, b_hi, dims, preferred_element_type=F32)
    if passes > 1:
        a_lo = (a - a_hi.astype(F32)).astype(BF16)
        b_lo = (b - b_hi.astype(F32)).astype(BF16)
        out = out + lax.dot_general(a_hi, b_lo, dims, preferred_element_type=F32)
        out = out + lax.dot_general(a_lo, b_hi, dims, preferred_element_type=F32)
    return out


@functools.partial(jax.custom_vjp, nondiff_argnums=(2,))
def nn(a, b, passes=1):
    return raw(a, b, NN, passes)


nn.defvjp(
    lambda a, b, p: (raw(a, b, NN, p), (a, b)),
    lambda p, kept, g: (raw(g, kept[1], NT, p), raw(kept[0], g, TN, p)),
)


@functools.partial(jax.custom_vjp, nondiff_argnums=(2,))
def nt(a, b, passes=1):
    return raw(a, b, NT, passes)


nt.defvjp(
    lambda a, b, p: (raw(a, b, NT, p), (a, b)),
    lambda p, kept, g: (raw(g, kept[1], NN, p), raw(g, kept[0], TN, p)),
)


@functools.partial(jax.custom_vjp, nondiff_argnums=(2,))
def tn(a, b, passes=1):
    return raw(a, b, TN, passes)


tn.defvjp(
    lambda a, b, p: (raw(a, b, TN, p), (a, b)),
    lambda p, kept, g: (raw(kept[1], g, NT, p), raw(kept[0], g, NN, p)),
)


def lower_ones():
    rows = lax.broadcasted_iota(jnp.int32, (CHUNK, CHUNK), 0)
    columns = lax.broadcasted_iota(jnp.int32, (CHUNK, CHUNK), 1)
    return jnp.where(rows >= columns, 1.0, 0.0)


def split3(v):
    hi = v.astype(BF16)
    rest = v - hi.astype(F32)
    mid = rest.astype(BF16)
    return hi, mid, (rest - mid.astype(F32)).astype(BF16)


@jax.custom_vjp
def running(v):
    ones = lower_ones().astype(BF16)
    return sum(lax.dot_general(ones, piece, NN, preferred_element_type=F32) for piece in split3(v))


def running_back(kept, g):
    ones = lower_ones().astype(BF16)
    return (sum(lax.dot_general(ones, piece, TN, preferred_element_type=F32) for piece in split3(g)),)


running.defvjp(lambda v: (running(v), None), running_back)


def inverse_value(lower):
    rows = lax.broadcasted_iota(jnp.int32, (CHUNK, CHUNK), 0)
    columns = lax.broadcasted_iota(jnp.int32, (CHUNK, CHUNK), 1)
    result = jnp.where(rows == columns, 1.0, 0.0)
    size = 1
    while size < CHUNK:
        joined = (rows // (2 * size) == columns // (2 * size)) & (rows // size != columns // size)
        between = jnp.where(joined, lower, 0.0)
        if size == 1:
            result = result - between
        else:
            result = result - raw(result, raw(between, result, NN, 3), NN, 3)
        size *= 2
    return result


@jax.custom_vjp
def inverse(lower):
    return inverse_value(lower)


def inverse_keep(lower):
    value = inverse_value(lower)
    return value, value


def inverse_back(value, g):
    return (-raw(raw(value, g, TN, 1), value, NT, 1),)


inverse.defvjp(inverse_keep, inverse_back)


def roll_rows(v, distance):
    if KERNELS:
        return pltpu.roll(v, distance, 0)
    return jnp.roll(v, distance, 0)


@functools.partial(jax.custom_vjp, nondiff_argnums=(1,))
def shift_rows(v, distance):
    rows = lax.broadcasted_iota(jnp.int32, v.shape, 0)
    return jnp.where(rows >= distance, roll_rows(v, distance), 0.0)


def shift_back(distance, kept, g):
    rows = lax.broadcasted_iota(jnp.int32, g.shape, 0)
    return (jnp.where(rows < g.shape[0] - distance, roll_rows(g, g.shape[0] - distance), 0.0),)


shift_rows.defvjp(lambda v, d: (shift_rows(v, d), None), shift_back)


@jax.custom_vjp
def split_rows(v):
    return tuple(v[i : i + CHUNK] for i in range(0, v.shape[0], CHUNK))


split_rows.defvjp(lambda v: (split_rows(v), None), lambda kept, g: (jnp.concatenate(g, axis=0),))


@jax.custom_vjp
def low(v):
    return v.astype(BF16).astype(F32)


low.defvjp(lambda v: (low(v), None), lambda kept, g: (g,))


@jax.custom_vjp
def softplus(v):
    return jnp.maximum(v, 0.0) + jnp.log1p(jnp.exp(-jnp.abs(v)))


softplus.defvjp(lambda v: (softplus(v), v), lambda v, g: (g * jax.nn.sigmoid(v),))


def silu(v):
    return v * jax.nn.sigmoid(v)


def unit_norm(v):
    return v * lax.rsqrt(jnp.sum(v * v, axis=-1, keepdims=True) + EPS)


def convolve(rows_in, taps):
    total = taps[KW - 1] * rows_in
    for j in range(KW - 1):
        total = total + taps[j] * shift_rows(rows_in, KW - 1 - j)
    return total


def recurrence(x_q, x_k, x_v, decay_raw, strength_raw, taps_q, taps_k, taps_v, decay_log, decay_bias):
    queries = low(unit_norm(silu(convolve(x_q, taps_q))) * DK**-0.5)
    keys = low(unit_norm(silu(convolve(x_k, taps_k))))
    values = low(silu(convolve(x_v, taps_v)))
    strength = jax.nn.sigmoid(strength_raw)
    log_decay = -jnp.exp(decay_log) * softplus(decay_raw + decay_bias)
    rows = lax.broadcasted_iota(jnp.int32, (CHUNK, CHUNK), 0)
    columns = lax.broadcasted_iota(jnp.int32, (CHUNK, CHUNK), 1)
    state = jnp.zeros((DK, x_v.shape[1]), F32)
    out = []
    for q, k, v, beta, ld in zip(*(split_rows(a) for a in (queries, keys, values, strength, log_decay))):
        total = running(jnp.broadcast_to(ld, (CHUNK, CHUNK)))
        whole = jnp.sum(ld, axis=0, keepdims=True)
        spread = total - total.T
        within = jnp.where(rows >= columns, jnp.exp(jnp.where(rows >= columns, spread, 0.0)), 0.0)
        below = jnp.where(rows > columns, within, 0.0)
        grown = jnp.exp(total)
        solve = inverse(beta * nt(k, k) * below)
        part_v = nn(solve, beta * v)
        part_k = nn(solve, beta * k * grown)
        scores = nt(q, k) * within
        fixed = part_v - nn(part_k, state)
        out.append(nn(q * grown, state) + nn(scores, fixed))
        state = jnp.exp(whole) * state + tn(k * jnp.exp(whole - total), fixed)
    return jnp.concatenate(out, axis=0)


def unpack(mixed, params, width):
    x = mixed[:, : 2 * DK + width].astype(F32)
    first = 2 * DK + width
    rates = mixed[:, first : first + 4].astype(F32)
    decay_raw = rates[:, 0:1] + rates[:, 1:2]
    strength_raw = rates[:, 2:3] + rates[:, 3:4]
    taps_q = [params[j : j + 1, :DK] for j in range(KW)]
    taps_k = [params[j : j + 1, DK : 2 * DK] for j in range(KW)]
    taps_v = [params[j : j + 1, 2 * DK : 2 * DK + width] for j in range(KW)]
    return (
        x[:, :DK],
        x[:, DK : 2 * DK],
        x[:, 2 * DK :],
        decay_raw,
        strength_raw,
        taps_q,
        taps_k,
        taps_v,
        params[KW : KW + 1, 0:1],
        params[KW + 1 : KW + 2, 0:1],
    )


def recur_forward(mixed, params, width):
    return recurrence(*unpack(mixed, params, width)).astype(BF16)


def recur_backward(mixed, params, grad_out, width):
    unused, back = jax.vjp(recurrence, *unpack(mixed, params, width))
    g_q, g_k, g_v, g_decay, g_strength, g_tq, g_tk, g_tv, g_log, g_bias = back(grad_out.astype(F32))
    wide = mixed.shape[1]
    count = mixed.shape[0]
    lane = lax.broadcasted_iota(jnp.int32, (count, wide - 2 * DK - width), 1)

    def halves(v):
        hi = v.astype(BF16).astype(F32)
        return hi, v - hi

    tail = jnp.zeros(lane.shape, F32)
    for index, piece in enumerate(halves(g_decay) + halves(g_strength)):
        tail = jnp.where(lane == index, piece, tail)
    grad_mixed = jnp.concatenate([g_q, g_k, g_v, tail], axis=1).astype(BF16)
    pad = wide - 2 * DK - width
    rows = [
        jnp.concatenate([g_tq[j], g_tk[j], g_tv[j], jnp.zeros((1, pad), F32)], axis=1)
        for j in range(KW)
    ]
    rows.append(jnp.broadcast_to(g_log, (1, wide)))
    rows.append(jnp.broadcast_to(g_bias, (1, wide)))
    rows.append(jnp.zeros((2, wide), F32))
    return grad_mixed, jnp.concatenate(rows, axis=0)


def forward_kernel(width, mixed_ref, params_ref, out_ref):
    out_ref[...] = recur_forward(mixed_ref[...], params_ref[...], width)


def backward_kernel(width, mixed_ref, params_ref, grad_ref, out_ref, small_ref):
    out_ref[...], small_ref[...] = recur_backward(
        mixed_ref[...], params_ref[...], grad_ref[...], width
    )


LIMIT = 48 * 1024 * 1024


def call_forward(mixed, params, width):
    if not KERNELS:
        return recur_forward(mixed, params, width)
    return pl.pallas_call(
        functools.partial(forward_kernel, width),
        out_shape=jax.ShapeDtypeStruct((mixed.shape[0], width), BF16),
        compiler_params=pltpu.CompilerParams(vmem_limit_bytes=LIMIT),
        name="recur_forward",
    )(mixed, params)


def call_backward(mixed, params, grad_out, width):
    if not KERNELS:
        return recur_backward(mixed, params, grad_out, width)
    return pl.pallas_call(
        functools.partial(backward_kernel, width),
        out_shape=(
            jax.ShapeDtypeStruct(mixed.shape, BF16),
            jax.ShapeDtypeStruct(params.shape, F32),
        ),
        compiler_params=pltpu.CompilerParams(vmem_limit_bytes=LIMIT),
        name="recur_backward",
    )(mixed, params, grad_out)


def dot(a, b, dims=NN):
    return lax.dot_general(a, b, dims, preferred_element_type=F32)


def norm_scale(v, eps):
    return lax.rsqrt(jnp.mean(v * v, axis=-1, keepdims=True) + eps)


def norm_back(v, scale, gain, grad):
    gained = gain * grad
    mean = jnp.mean(gained * v, axis=-1, keepdims=True)
    grad_v = scale * gained - v * (scale * scale * scale) * mean
    return grad_v, jnp.sum(grad * v * scale, axis=0)


def silu_grad(v):
    s = jax.nn.sigmoid(v)
    return s * (1.0 + v * (1.0 - s))


def body(
    inputs,
    cotangent,
    gains,
    w_in,
    w_rates,
    a_log,
    dt_bias,
    conv_kernel,
    out_gain,
    w_out,
    w_ffn_in,
    w_down,
):
    core = lax.axis_index("section")
    place = lax.axis_index("seq")
    parts = lax.axis_size("seq")
    micro, rows, features = inputs.shape
    heads = w_in.shape[2]
    columns = w_in.shape[3]
    qkv = 2 * DK + DV
    hidden_width = w_ffn_in.shape[3]
    splits = parts // heads
    width = DV // splits
    wide = -(-(2 * DK + width + 4) // LANES) * LANES
    own_head = place // splits
    own_split = place % splits
    slab = features // parts
    half = slab // 2

    def pair(own):
        other = swap_section(own)
        return (jnp.where(core == 0, own, other), jnp.where(core == 0, other, own))

    w_project = pair(w_in[0].reshape(features, heads * columns))
    rate_rows = jnp.transpose(w_rates[0], (0, 2, 1)).reshape(2 * heads, features)
    w_rate = pair(jnp.pad(rate_rows, ((0, 16 - 2 * heads), (0, 0))))
    flat = jnp.concatenate(
        [
            gains[0].reshape(-1),
            conv_kernel[0].reshape(-1),
            jnp.pad(jnp.concatenate([out_gain[0], a_log[0], dt_bias[0]]), (0, 1024 - DV - 2 * heads)),
        ]
    ).reshape(-1, LANES)
    flats = pair(flat)
    w_mix = pair(w_out[0].reshape(heads * DV, features))
    w_hidden = pair(jnp.transpose(w_ffn_in[0], (1, 2, 0)).reshape(2 * hidden_width, features))
    w_back = pair(w_down[0])

    def small_params(index):
        v = flats[index].reshape(-1)
        gain_mix = v[:features].reshape(1, features)
        gain_ffn = v[features : 2 * features].reshape(1, features)
        at = 2 * features
        taps = v[at : at + KW * heads * qkv].reshape(KW, heads, qkv)
        at += KW * heads * qkv
        gain_out = v[at : at + DV].reshape(1, DV)
        logs = v[at + DV : at + DV + heads]
        biases = v[at + DV + heads : at + DV + 2 * heads]
        taps = lax.dynamic_index_in_dim(taps, own_head, 1, keepdims=False)
        taps_v = lax.dynamic_slice_in_dim(taps, 2 * DK + own_split * width, width, 1)
        taps = jnp.concatenate(
            [taps[:, : 2 * DK], taps_v, jnp.zeros((KW, wide - 2 * DK - width), F32)], axis=1
        )
        log = lax.dynamic_index_in_dim(logs, own_head, 0, keepdims=False)
        bias = lax.dynamic_index_in_dim(biases, own_head, 0, keepdims=False)
        params = jnp.concatenate(
            [
                taps,
                jnp.full((1, wide), log),
                jnp.full((1, wide), bias),
                jnp.zeros((2, wide), F32),
            ],
            axis=0,
        )
        return gain_mix, gain_ffn, gain_out, params

    smalls = (small_params(0), small_params(1))

    def hi_lo(v):
        hi = v.astype(BF16)
        return hi, (v - hi.astype(F32)).astype(BF16)

    def per_split(value, h, j):
        return value[:, h * DV + j * width : h * DV + (j + 1) * width]

    def from_splits(received):
        return [
            jnp.concatenate([received[h * splits + j] for j in range(splits)], axis=1)
            for h in range(heads)
        ]

    def gather_rows(value):
        return lax.all_gather(value, "seq", axis=0, tiled=True)

    def forward(index, source):
        gain_mix, gain_ffn, gain_out, params = smalls[index]
        kept = {"source": source}
        normed = (source * norm_scale(source, EPS) * gain_mix).astype(BF16)
        projected = dot(normed, w_project[index])
        rates = dot(normed, w_rate[index], NT)
        sent = []
        for h in range(heads):
            at = h * columns
            pieces = hi_lo(rates[:, h : h + 1]) + hi_lo(rates[:, heads + h : heads + h + 1])
            tail = jnp.pad(
                jnp.concatenate(pieces, axis=1), ((0, 0), (0, wide - 2 * DK - width - 4))
            )
            for j in range(splits):
                v_at = at + 2 * DK + j * width
                sent.append(
                    jnp.concatenate(
                        [
                            projected[:, at : at + 2 * DK].astype(BF16),
                            projected[:, v_at : v_at + width].astype(BF16),
                            tail,
                        ],
                        axis=1,
                    )
                )
        mixed = exchange_seq(jnp.stack(sent)).reshape(parts * rows, wide)
        recurrent = call_forward(mixed, params, width)
        outs = from_splits(exchange_seq(recurrent.reshape(parts, rows, width)))
        outs = [o.astype(F32) for o in outs]
        gates = [projected[:, h * columns + qkv : (h + 1) * columns] for h in range(heads)]
        gated = jnp.concatenate(
            [
                (o * norm_scale(o, HEAD_EPS) * gain_out * silu(g)).astype(BF16)
                for o, g in zip(outs, gates)
            ],
            axis=1,
        )
        hidden = source + sum_heads(dot(gated, w_mix[index]))
        hidden_norm = (hidden * norm_scale(hidden, EPS) * gain_ffn).astype(BF16)
        gate_up = dot(hidden_norm, w_hidden[index], NT)
        gate, up = gate_up[:, :hidden_width], gate_up[:, hidden_width:]
        active = (silu(gate) * up).astype(BF16)
        result = (hidden + sum_heads(dot(active, w_back[index]))).astype(BF16)
        kept.update(
            normed=normed,
            mixed=mixed,
            outs=outs,
            gates=gates,
            gated=gated,
            hidden=hidden,
            hidden_norm=hidden_norm,
            gate=gate,
            up=up,
            active=active,
            normed_all=gather_rows(normed),
        )
        return result, kept

    def by_core(value):
        cut = value.reshape(value.shape[0], parts, 2, half)
        mine = jnp.where(core == 0, cut[:, :, 0], cut[:, :, 1])
        others = jnp.where(core == 0, cut[:, :, 1], cut[:, :, 0])
        return mine.reshape(-1, parts * half), others.reshape(-1, parts * half)

    def weight_grads(pairs):
        sums = []
        for left, right in pairs:
            mine, others = by_core(right)
            left_all = jnp.concatenate([left, swap_section(left)], axis=0)
            right_all = jnp.concatenate([mine, swap_section(others)], axis=0)
            product = lax.dot_general(
                left_all, right_all.reshape(-1, parts, half), TN, preferred_element_type=F32
            )
            sums.append(jnp.transpose(product, (1, 0, 2)).astype(BF16))
        whole = jnp.concatenate(sums, axis=1)
        return lax.psum_scatter(whole, "seq", scatter_dimension=0, tiled=False)

    def backward(index, upstream, kept):
        gain_mix, gain_ffn, gain_out, params = smalls[index]
        up_low = upstream.astype(BF16)
        grad_active = dot(up_low, w_back[index], NT)
        gate, up = kept["gate"], kept["up"]
        grad_gate_up = jnp.concatenate(
            [grad_active * up * silu_grad(gate), grad_active * silu(gate)], axis=1
        ).astype(BF16)
        grad_hidden_norm = sum_heads(dot(grad_gate_up, w_hidden[index])).astype(BF16).astype(F32)
        ffn_sums = weight_grads(
            [(grad_gate_up, kept["hidden_norm"]), (kept["active"], up_low)]
        )
        hidden = kept["hidden"]
        grad_hidden, grad_gain_ffn = norm_back(
            hidden, norm_scale(hidden, EPS), gain_ffn, grad_hidden_norm
        )
        grad_stream = upstream + grad_hidden
        stream_low = grad_stream.astype(BF16)
        grad_gated = dot(stream_low, w_mix[index], NT)
        sent, grad_gates, grad_gain_out = [], [], 0.0
        for h in range(heads):
            out, gate_pre = kept["outs"][h], kept["gates"][h]
            g = grad_gated[:, h * DV : (h + 1) * DV]
            scale = norm_scale(out, HEAD_EPS)
            grad_gates.append((g * out * scale * gain_out * silu_grad(gate_pre)).astype(BF16))
            grad_out, grad_gain = norm_back(out, scale, gain_out, g * silu(gate_pre))
            grad_gain_out = grad_gain_out + grad_gain
            for j in range(splits):
                sent.append(grad_out[:, j * width : (j + 1) * width].astype(BF16))
        grad_all = exchange_seq(jnp.stack(sent)).reshape(parts * rows, width)
        grad_gates = jnp.concatenate(grad_gates, axis=1)
        mix_sums = weight_grads([(kept["gated"], stream_low), (grad_gates, kept["normed"])])
        grad_mixed, grad_params = call_backward(kept["mixed"], params, grad_all, width)
        returned = exchange_seq(grad_mixed.reshape(parts, rows, wide)).astype(F32)
        grad_project, grad_rates = [], []
        for h in range(heads):
            mine = returned[h * splits : (h + 1) * splits]
            summed = jnp.sum(mine[:, :, : 2 * DK], axis=0).astype(BF16)
            values = [mine[j, :, 2 * DK : 2 * DK + width].astype(BF16) for j in range(splits)]
            grad_project += [summed] + values + [grad_gates[:, h * DV : (h + 1) * DV]]
            tail = jnp.sum(mine[:, :, 2 * DK + width : 2 * DK + width + 4], axis=0)
            grad_rates.append((tail[:, 0:1] + tail[:, 1:2], tail[:, 2:3] + tail[:, 3:4]))
        grad_project = jnp.concatenate(grad_project, axis=1)
        grad_rates = jnp.concatenate(
            [r[0] for r in grad_rates] + [r[1] for r in grad_rates] + [jnp.zeros((rows, 16 - 2 * heads), F32)],
            axis=1,
        ).astype(BF16)
        part = dot(grad_project, w_project[index], NT) + dot(grad_rates, w_rate[index])
        extra = jnp.pad(grad_gain_out.reshape(1, DV), ((0, 15), (0, features - DV)))
        summed = sum_heads(jnp.concatenate([part, extra], axis=0))
        grad_normed = summed[:rows].astype(BF16).astype(F32)
        source = kept["source"]
        grad_source, grad_gain_mix = norm_back(
            source, norm_scale(source, EPS), gain_mix, grad_normed
        )
        grad_input = (grad_stream + grad_source).astype(BF16)
        product = dot(kept["normed_all"], grad_mixed, TN).reshape(parts, 2, half, wide)
        mine = jnp.where(core == 0, product[:, 0], product[:, 1])
        others = jnp.where(core == 0, product[:, 1], product[:, 0])
        mine = (mine + swap_section(others.astype(BF16)).astype(F32)).astype(BF16)
        project_sums = exchange_seq(mine)
        taps = jnp.zeros((KW, heads, qkv), F32)
        taps = lax.dynamic_update_slice(taps, grad_params[:KW, None, : 2 * DK], (0, own_head, 0))
        taps = lax.dynamic_update_slice(
            taps,
            grad_params[:KW, None, 2 * DK : 2 * DK + width],
            (0, own_head, 2 * DK + own_split * width),
        )
        one = jnp.arange(heads) == own_head
        logs = jnp.where(one, grad_params[KW, 0], 0.0)
        biases = jnp.where(one, grad_params[KW + 1, 0], 0.0)
        small = jnp.concatenate(
            [
                grad_gain_mix,
                grad_gain_ffn,
                taps.reshape(-1),
                jnp.pad(
                    jnp.concatenate([summed[rows, :DV], logs, biases]), (0, 1024 - DV - 2 * heads)
                ),
            ]
        ).reshape(-1, LANES)
        return grad_input, (ffn_sums, mix_sums, project_sums, small)

    pick = lambda a: jnp.where(core == 0, a[0], a[1])
    first, kept_first = forward(0, pick(inputs).astype(F32))
    final, kept_final = forward(1, first.astype(F32))
    grad_first, sums_final = backward(1, pick(cotangent).astype(F32), kept_final)
    grad_inputs, sums_first = backward(0, grad_first.astype(F32), kept_first)

    def settle(a_first, a_final):
        mine = jnp.where(core == 0, a_first, a_final)
        others = jnp.where(core == 0, a_final, a_first)
        return mine, swap_section(others)

    def joined(index, axis):
        mine, others = settle(sums_first[index], sums_final[index])
        lead = jnp.where(core == 0, mine, others)
        follow = jnp.where(core == 0, others, mine)
        return jnp.concatenate([lead, follow], axis=axis).astype(F32)

    ffn = joined(0, 1)
    mix = joined(1, 1)
    project = joined(2, 1)
    small_mine, small_others = settle(sums_first[3], sums_final[3])
    small = sum_seq(small_mine + small_others).reshape(-1)

    grad_hidden_w = jnp.transpose(ffn[: 2 * hidden_width].reshape(2, hidden_width, slab), (2, 0, 1))
    grad_back_w = ffn[2 * hidden_width :]
    grad_mix_w = mix[: heads * DV].reshape(heads, DV, slab)
    gate_columns = jnp.transpose(mix[heads * DV :]).reshape(slab, heads, DV)
    cut = project.reshape(heads, splits, slab, wide)
    qk = jnp.sum(cut[..., : 2 * DK], axis=1)
    vs = jnp.moveaxis(cut[..., 2 * DK : 2 * DK + width], 1, 2).reshape(heads, slab, DV)
    grad_project_w = jnp.concatenate(
        [jnp.transpose(qk, (1, 0, 2)), jnp.transpose(vs, (1, 0, 2)), gate_columns], axis=2
    )
    tail = jnp.sum(cut[..., 2 * DK + width : 2 * DK + width + 4], axis=1)
    grad_rate_w = jnp.stack([tail[..., 0] + tail[..., 1], tail[..., 2] + tail[..., 3]])
    grad_rate_w = jnp.transpose(grad_rate_w, (0, 2, 1))
    at = 2 * features
    grad_gains = small[:at].reshape(2, features)
    grad_taps = small[at : at + KW * heads * qkv].reshape(KW, heads, qkv)
    at += KW * heads * qkv
    grad_out_gain = small[at : at + DV]
    grad_log = small[at + DV : at + DV + heads]
    grad_bias = small[at + DV + heads : at + DV + 2 * heads]
    def both(first_rows, final_rows):
        mine = jnp.where(core == 0, first_rows, final_rows)
        others = swap_section(jnp.where(core == 0, final_rows, first_rows))
        lead = jnp.where(core == 0, mine, others)
        follow = jnp.where(core == 0, others, mine)
        return jnp.stack([lead, follow])

    block_out = both(first, final)
    input_grad = both(grad_inputs, grad_first)
    return (
        block_out[None],
        input_grad[None],
        grad_gains[None],
        grad_project_w[None],
        grad_rate_w[None],
        grad_log[None],
        grad_bias[None],
        grad_taps[None],
        grad_out_gain[None],
        grad_mix_w[None],
        grad_hidden_w[None],
        grad_back_w[None],
    )


def solution(mesh):
    placed = (
        P(None, "seq", None),
        P(None, "seq", None),
        P("section", None, None),
        P("section", None, "head", None),
        P("section", None, None, "head"),
        P("section", "head"),
        P("section", "head"),
        P("section", None, "head", None),
        P("section", None),
        P("section", "head", None, None),
        P("section", None, None, "head"),
        P("section", "head", None),
    )
    return jax.shard_map(
        body,
        mesh=mesh,
        in_specs=placed,
        out_specs=(
            P("section", None, "seq", None),
            P("section", None, "seq", None),
            P("section", None, None),
            P("section", "seq", "head", None),
            P("section", None, "seq", "head"),
            P("section", "head"),
            P("section", "head"),
            P("section", None, "head", None),
            P("section", None),
            P("section", "head", None, "seq"),
            P("section", "seq", None, "head"),
            P("section", "head", "seq"),
        ),
        check_vma=False,
    )
```

```python
import functools
import math

import jax
import jax.numpy as jnp
from jax import lax
from jax.experimental import pallas as pl
from jax.experimental.pallas import tpu as pltpu
from jax.sharding import PartitionSpec as P

DK = 128
DV = 256
KW = 4
CHUNK = 128
LANES = 128
EPS = 1e-06
HEAD_EPS = 0.01
AXES = ("section", "seq", "head")
KERNELS = True
F32 = jnp.float32
BF16 = jnp.bfloat16


def route(move):
    sections, seqs, heads = (lax.axis_size(axis) for axis in AXES)
    pairs = []
    for s in range(sections):
        for z in range(seqs):
            for h in range(heads):
                s2, z2, h2 = move(s, z, h)
                pairs.append(((s * seqs + z) * heads + h, (s2 * seqs + z2) * heads + h2))
    return pairs


def swap_section(value):
    return lax.ppermute(value, AXES, route(lambda s, z, h: (1 - s, z, h)))


def sum_heads(part):
    total = part.astype(BF16)
    size = lax.axis_size("head")
    steps = [1 << i for i in range(size.bit_length() - 1)]
    for i, step in enumerate(steps):
        back = steps[-1 - i]
        other = lax.ppermute(total, AXES, route(lambda s, z, h: (s, z, h ^ (step if s == 0 else back))))
        if i + 1 == len(steps):
            return total, other
        total = (total.astype(F32) + other.astype(F32)).astype(BF16)


def after(value, *first):
    return lax.optimization_barrier((value,) + first)[0]


def sum_seq(part):
    total = part
    step = 1
    while step < lax.axis_size("seq"):
        total = total + lax.ppermute(total, AXES, route(lambda s, z, h: (s, z ^ step, h)))
        step *= 2
    return total


def exchange_seq(value):
    return lax.all_to_all(value, "seq", 0, 0, tiled=False)


NN = (((1,), (0,)), ((), ()))
NT = (((1,), (1,)), ((), ()))
TN = (((0,), (0,)), ((), ()))


def raw(a, b, dims, passes):
    a_hi, b_hi = a.astype(BF16), b.astype(BF16)
    out = lax.dot_general(a_hi, b_hi, dims, preferred_element_type=F32)
    if passes > 1:
        a_lo = (a - a_hi.astype(F32)).astype(BF16)
        b_lo = (b - b_hi.astype(F32)).astype(BF16)
        out = out + lax.dot_general(a_hi, b_lo, dims, preferred_element_type=F32)
        out = out + lax.dot_general(a_lo, b_hi, dims, preferred_element_type=F32)
    return out


@functools.partial(jax.custom_vjp, nondiff_argnums=(2,))
def nn(a, b, passes=1):
    return raw(a, b, NN, passes)


nn.defvjp(
    lambda a, b, p: (raw(a, b, NN, p), (a, b)),
    lambda p, kept, g: (raw(g, kept[1], NT, p), raw(kept[0], g, TN, p)),
)


@functools.partial(jax.custom_vjp, nondiff_argnums=(2,))
def nt(a, b, passes=1):
    return raw(a, b, NT, passes)


nt.defvjp(
    lambda a, b, p: (raw(a, b, NT, p), (a, b)),
    lambda p, kept, g: (raw(g, kept[1], NN, p), raw(g, kept[0], TN, p)),
)


@functools.partial(jax.custom_vjp, nondiff_argnums=(2,))
def tn(a, b, passes=1):
    return raw(a, b, TN, passes)


tn.defvjp(
    lambda a, b, p: (raw(a, b, TN, p), (a, b)),
    lambda p, kept, g: (raw(kept[1], g, NT, p), raw(kept[0], g, NN, p)),
)


def lower_ones():
    rows = lax.broadcasted_iota(jnp.int32, (CHUNK, CHUNK), 0)
    columns = lax.broadcasted_iota(jnp.int32, (CHUNK, CHUNK), 1)
    return jnp.where(rows >= columns, 1.0, 0.0)


def split3(v):
    hi = v.astype(BF16)
    rest = v - hi.astype(F32)
    mid = rest.astype(BF16)
    return hi, mid, (rest - mid.astype(F32)).astype(BF16)


@jax.custom_vjp
def running(v):
    ones = lower_ones().astype(BF16)
    return sum(lax.dot_general(ones, piece, NN, preferred_element_type=F32) for piece in split3(v))


def running_back(kept, g):
    ones = lower_ones().astype(BF16)
    return (sum(lax.dot_general(ones, piece, TN, preferred_element_type=F32) for piece in split3(g)),)


running.defvjp(lambda v: (running(v), None), running_back)


def inverse_value(lowers):
    rows = lax.broadcasted_iota(jnp.int32, (CHUNK, CHUNK), 0)
    columns = lax.broadcasted_iota(jnp.int32, (CHUNK, CHUNK), 1)
    results = [jnp.where(rows == columns, 1.0, 0.0)] * len(lowers)
    size = 1
    while size < CHUNK:
        joined = (rows // (2 * size) == columns // (2 * size)) & (rows // size != columns // size)
        between = [jnp.where(joined, lower, 0.0) for lower in lowers]
        if size == 1:
            results = [r - b for r, b in zip(results, between)]
        else:
            middle = [raw(b, r, NN, 3) for r, b in zip(results, between)]
            results = [r - raw(r, m, NN, 3) for r, m in zip(results, middle)]
        size *= 2
    return tuple(results)


@jax.custom_vjp
def inverse(lowers, values):
    return inverse_value(lowers) if values is None else values


def inverse_keep(lowers, values):
    values = inverse(lowers, values)
    return values, values


def inverse_back(values, grads):
    first = [raw(value, g, TN, 1) for value, g in zip(values, grads)]
    return tuple(-raw(f, value, NT, 1) for f, value in zip(first, values)), None


inverse.defvjp(inverse_keep, inverse_back)


def roll_rows(v, distance):
    if KERNELS:
        return pltpu.roll(v, distance, 0)
    return jnp.roll(v, distance, 0)


@functools.partial(jax.custom_vjp, nondiff_argnums=(1,))
def shift_rows(v, distance):
    rows = lax.broadcasted_iota(jnp.int32, v.shape, 0)
    return jnp.where(rows >= distance, roll_rows(v, distance), 0.0)


def shift_back(distance, kept, g):
    rows = lax.broadcasted_iota(jnp.int32, g.shape, 0)
    return (jnp.where(rows < g.shape[0] - distance, roll_rows(g, g.shape[0] - distance), 0.0),)


shift_rows.defvjp(lambda v, d: (shift_rows(v, d), None), shift_back)


@jax.custom_vjp
def split_rows(v):
    return tuple(v[i : i + CHUNK] for i in range(0, v.shape[0], CHUNK))


split_rows.defvjp(lambda v: (split_rows(v), None), lambda kept, g: (jnp.concatenate(g, axis=0),))


@jax.custom_vjp
def low(v):
    return v.astype(BF16).astype(F32)


low.defvjp(lambda v: (low(v), None), lambda kept, g: (g,))


@jax.custom_vjp
def softplus(v):
    return jnp.maximum(v, 0.0) + jnp.log1p(jnp.exp(-jnp.abs(v)))


softplus.defvjp(lambda v: (softplus(v), v), lambda v, g: (g * jax.nn.sigmoid(v),))


def silu(v):
    return v * jax.nn.sigmoid(v)


def unit_norm(v):
    return v * lax.rsqrt(jnp.sum(v * v, axis=-1, keepdims=True) + EPS)


def convolve(rows_in, taps):
    total = taps[KW - 1] * rows_in
    for j in range(KW - 1):
        total = total + taps[j] * shift_rows(rows_in, KW - 1 - j)
    return total


def recurrence(
    x_q, x_k, x_v, decay_raw, strength_raw, taps_q, taps_k, taps_v, decay_log, decay_bias, solves=None
):
    queries = low(unit_norm(silu(convolve(x_q, taps_q))) * DK**-0.5)
    keys = low(unit_norm(silu(convolve(x_k, taps_k))))
    values = low(silu(convolve(x_v, taps_v)))
    strength = jax.nn.sigmoid(strength_raw)
    log_decay = -jnp.exp(decay_log) * softplus(decay_raw + decay_bias)
    rows = lax.broadcasted_iota(jnp.int32, (CHUNK, CHUNK), 0)
    columns = lax.broadcasted_iota(jnp.int32, (CHUNK, CHUNK), 1)
    queries, keys, values, strength, log_decay = (
        split_rows(a) for a in (queries, keys, values, strength, log_decay)
    )
    chunks = range(len(keys))
    totals = [running(jnp.broadcast_to(ld, (CHUNK, CHUNK))) for ld in log_decay]
    wholes = [jnp.sum(ld, axis=0, keepdims=True) for ld in log_decay]
    within = []
    for total in totals:
        spread = total - total.T
        within.append(
            jnp.where(rows >= columns, jnp.exp(jnp.where(rows >= columns, spread, 0.0)), 0.0)
        )
    grown = [jnp.exp(total) for total in totals]
    weighted = [strength[i] * keys[i] for i in chunks]
    lowers = tuple(
        strength[i] * nt(keys[i], keys[i]) * jnp.where(rows > columns, within[i], 0.0)
        for i in chunks
    )
    solve = inverse(lowers, solves)
    part_v = [nn(solve[i], strength[i] * values[i]) for i in chunks]
    part_k = [nn(solve[i], weighted[i] * grown[i]) for i in chunks]
    scores = [nt(queries[i], keys[i]) * within[i] for i in chunks]
    ending = [keys[i] * jnp.exp(wholes[i] - totals[i]) for i in chunks]
    seen = [queries[i] * grown[i] - nn(scores[i], part_k[i]) for i in chunks]
    own = [nn(scores[i], part_v[i]) for i in chunks]
    forget = [tn(ending[i], part_k[i]) for i in chunks]
    learn = [tn(ending[i], part_v[i]) for i in chunks]
    state = jnp.zeros((DK, x_v.shape[1]), F32)
    out = []
    for i in chunks:
        out.append(nn(seen[i], state) + own[i])
        state = jnp.exp(wholes[i]) * state + learn[i] - nn(forget[i], state)
    return jnp.concatenate(out, axis=0), solve


def unpack(mixed, params, width):
    x = mixed[:, : 2 * DK + width].astype(F32)
    first = 2 * DK + width
    rates = mixed[:, first : first + 4].astype(F32)
    decay_raw = rates[:, 0:1] + rates[:, 1:2]
    strength_raw = rates[:, 2:3] + rates[:, 3:4]
    taps_q = [params[j : j + 1, :DK] for j in range(KW)]
    taps_k = [params[j : j + 1, DK : 2 * DK] for j in range(KW)]
    taps_v = [params[j : j + 1, 2 * DK : 2 * DK + width] for j in range(KW)]
    return (
        x[:, :DK],
        x[:, DK : 2 * DK],
        x[:, 2 * DK :],
        decay_raw,
        strength_raw,
        taps_q,
        taps_k,
        taps_v,
        params[KW : KW + 1, 0:1],
        params[KW + 1 : KW + 2, 0:1],
    )


def recur_forward(mixed, params, width):
    out, solve = recurrence(*unpack(mixed, params, width))
    return out.astype(BF16), jnp.concatenate(solve, axis=0).astype(BF16)


def recur_backward(mixed, params, solves, grad_out, width):
    solves = tuple(v.astype(F32) for v in split_rows(solves))
    unused, back = jax.vjp(
        lambda *a: recurrence(*a, solves=solves)[0], *unpack(mixed, params, width)
    )
    g_q, g_k, g_v, g_decay, g_strength, g_tq, g_tk, g_tv, g_log, g_bias = back(grad_out.astype(F32))
    wide = mixed.shape[1]
    count = mixed.shape[0]
    lane = lax.broadcasted_iota(jnp.int32, (count, wide - 2 * DK - width), 1)

    def halves(v):
        hi = v.astype(BF16).astype(F32)
        return hi, v - hi

    tail = jnp.zeros(lane.shape, F32)
    for index, piece in enumerate(halves(g_decay) + halves(g_strength)):
        tail = jnp.where(lane == index, piece, tail)
    grad_mixed = jnp.concatenate([g_q, g_k, g_v, tail], axis=1).astype(BF16)
    pad = wide - 2 * DK - width
    rows = [
        jnp.concatenate([g_tq[j], g_tk[j], g_tv[j], jnp.zeros((1, pad), F32)], axis=1)
        for j in range(KW)
    ]
    rows.append(jnp.broadcast_to(g_log, (1, wide)))
    rows.append(jnp.broadcast_to(g_bias, (1, wide)))
    rows.append(jnp.zeros((2, wide), F32))
    return grad_mixed, jnp.concatenate(rows, axis=0)


def dot(a, b, dims=NN):
    return lax.dot_general(a, b, dims, preferred_element_type=F32)


def norm_scale(v, eps):
    return lax.rsqrt(jnp.mean(v * v, axis=-1, keepdims=True) + eps)


def norm_back(v, scale, gain, grad):
    gained = gain * grad
    mean = jnp.mean(gained * v, axis=-1, keepdims=True)
    grad_v = scale * gained - v * (scale * scale * scale) * mean
    return grad_v, jnp.sum(grad * v * scale, axis=0, keepdims=True)


def silu_grad(v):
    s = jax.nn.sigmoid(v)
    return s * (1.0 + v * (1.0 - s))


def local(function, shapes, operands, flops, name, limit=28):
    if not KERNELS:
        return function(*operands)
    count = len(operands)

    def kernel(*refs):
        results = function(*[ref[...] for ref in refs[:count]])
        for ref, result in zip(refs[count:], results):
            ref[...] = result

    moved = sum(math.prod(a.shape) * a.dtype.itemsize for a in (*operands, *shapes))
    return pl.pallas_call(
        kernel,
        out_shape=shapes,
        compiler_params=pltpu.CompilerParams(vmem_limit_bytes=limit * 1024 * 1024),
        cost_estimate=pl.CostEstimate(flops=flops, bytes_accessed=moved, transcendentals=0),
        name=name,
    )(*operands)


def body(
    inputs,
    cotangent,
    gains,
    w_in,
    w_rates,
    a_log,
    dt_bias,
    conv_kernel,
    out_gain,
    w_out,
    w_ffn_in,
    w_down,
):
    core = lax.axis_index("section")
    place = lax.axis_index("seq")
    parts = lax.axis_size("seq")
    micro, rows, features = inputs.shape
    heads = w_in.shape[2]
    columns = w_in.shape[3]
    qkv = 2 * DK + DV
    hidden_width = w_ffn_in.shape[3]
    splits = parts // heads
    width = DV // splits
    wide = -(-(2 * DK + width + 4) // LANES) * LANES
    first_rate = 2 * DK + width
    own_head = place // splits
    own_split = place % splits
    slab = features // parts
    half = slab // 2
    shape = jax.ShapeDtypeStruct

    def pair(own):
        other = swap_section(own)
        return (jnp.where(core == 0, own, other), jnp.where(core == 0, other, own))

    w_project = pair(w_in[0].reshape(features, heads * columns))
    rate_rows = jnp.transpose(w_rates[0], (0, 2, 1)).reshape(2 * heads, features)
    w_rate = pair(jnp.pad(rate_rows, ((0, 16 - 2 * heads), (0, 0))))
    logs = jnp.concatenate([out_gain[0], a_log[0], dt_bias[0]])
    flats = pair(
        jnp.concatenate(
            [
                gains[0],
                conv_kernel[0].reshape(KW, heads * qkv),
                jnp.pad(logs, (0, features - DV - 2 * heads)).reshape(1, features),
                jnp.zeros((1, features), F32),
            ],
            axis=0,
        )
    )
    w_mix = pair(w_out[0].reshape(heads * DV, features))
    w_hidden = pair(jnp.transpose(w_ffn_in[0], (1, 2, 0)).reshape(2 * hidden_width, features))
    w_back = pair(w_down[0])

    def small_params(index):
        flat = flats[index]
        logs = flat[KW + 2 : KW + 3]
        taps = flat[2 : KW + 2].reshape(KW, heads, qkv)
        taps = lax.dynamic_index_in_dim(taps, own_head, 1, keepdims=False)
        taps_v = lax.dynamic_slice_in_dim(taps, 2 * DK + own_split * width, width, 1)
        log = lax.dynamic_index_in_dim(logs[0, DV : DV + heads], own_head, 0, keepdims=False)
        bias = lax.dynamic_index_in_dim(
            logs[0, DV + heads : DV + 2 * heads], own_head, 0, keepdims=False
        )
        params = jnp.concatenate(
            [
                jnp.concatenate([taps[:, : 2 * DK], taps_v, jnp.zeros((KW, wide - first_rate), F32)], axis=1),
                jnp.full((1, wide), log),
                jnp.full((1, wide), bias),
                jnp.zeros((2, wide), F32),
            ],
            axis=0,
        )
        return flat[0:1], flat[1:2], logs[:, :DV], params

    smalls = (small_params(0), small_params(1))

    flag = jnp.broadcast_to(jnp.where(core == 0, 1.0, 0.0).astype(F32), (1, LANES))

    def by_core(flag_now, value):
        first = jnp.broadcast_to(flag_now[:, :half], (value.shape[0], half)) > 0.5
        mine, others = [], []
        for p in range(parts):
            a = value[:, p * slab : p * slab + half].astype(F32)
            b = value[:, p * slab + half : (p + 1) * slab].astype(F32)
            mine.append(jnp.where(first, a, b))
            others.append(jnp.where(first, b, a))
        return [jnp.concatenate(v, axis=1).astype(BF16) for v in (mine, others)]

    halves = (shape((rows, parts * half), BF16),) * 2

    def hi_lo(v):
        hi = v.astype(BF16).astype(F32)
        return hi, v - hi

    def outs_of(received, h):
        return jnp.concatenate([received[h * splits + j] for j in range(splits)], axis=1).astype(F32)

    def front(flag_now, gain, w_proj, w_rate_now, *addends):
        source = addends[0].astype(F32)
        for addend in addends[1:]:
            source = source + addend.astype(F32)
        source_low = source.astype(BF16)
        source = source_low.astype(F32)
        normed = (source * norm_scale(source, EPS) * gain).astype(BF16)
        projected = dot(normed, w_proj)
        rates = dot(normed, w_rate_now, NT)
        lane = lax.broadcasted_iota(jnp.int32, (rows, wide - first_rate), 1)
        sent, gates = [], []
        for h in range(heads):
            at = h * columns
            tail = jnp.zeros(lane.shape, F32)
            pieces = hi_lo(rates[:, h : h + 1]) + hi_lo(rates[:, heads + h : heads + h + 1])
            for index, piece in enumerate(pieces):
                tail = jnp.where(lane == index, piece, tail)
            for j in range(splits):
                v_at = at + 2 * DK + j * width
                sent.append(
                    jnp.concatenate(
                        [projected[:, at : at + 2 * DK], projected[:, v_at : v_at + width], tail],
                        axis=1,
                    ).astype(BF16)
                )
            gates.append(projected[:, at + qkv : at + columns])
        return source_low, normed, jnp.stack(sent), jnp.concatenate(gates, axis=1), *by_core(flag_now, normed)

    def mix(gain_out, w_mix_now, received, gates):
        gated = []
        for h in range(heads):
            out = outs_of(received, h)
            gate = gates[:, h * DV : (h + 1) * DV]
            gated.append((out * norm_scale(out, HEAD_EPS) * gain_out * silu(gate)).astype(BF16))
        gated = jnp.concatenate(gated, axis=1)
        return gated, dot(gated, w_mix_now).astype(BF16)

    def ffn(flag_now, gain, w_hidden_now, w_back_now, source, one, two):
        hidden = source.astype(F32) + (one.astype(F32) + two.astype(F32))
        hidden_norm = (hidden * norm_scale(hidden, EPS) * gain).astype(BF16)
        gate = dot(hidden_norm, w_hidden_now[:hidden_width], NT)
        up = dot(hidden_norm, w_hidden_now[hidden_width:], NT)
        active = (silu(gate) * up).astype(BF16)
        part = dot(active, w_back_now).astype(BF16)
        return hidden, gate, up, active, part, *by_core(flag_now, hidden_norm)

    def forward(index, addends):
        gain_mix, gain_ffn, gain_out, params = smalls[index]
        source, normed, sent, gates, *normed_halves = local(
            front,
            (
                shape((rows, features), BF16),
                shape((rows, features), BF16),
                shape((parts, rows, wide), BF16),
                shape((rows, heads * DV), F32),
                *halves,
            ),
            (flag, gain_mix, w_project[index], w_rate[index], *addends),
            2 * rows * features * heads * columns,
            "front",
        )
        mixed = exchange_seq(sent).reshape(parts * rows, wide)
        recurrent, solves = local(
            lambda m, p: recur_forward(m, p, width),
            (shape((parts * rows, width), BF16), shape((parts * rows, CHUNK), BF16)),
            (mixed, params),
            20 * 2 * parts * rows * DK * DK,
            "recur_forward",
            28 if parts * rows <= 512 else 60,
        )
        received = exchange_seq(recurrent.reshape(parts, rows, width))
        gated, part = local(
            mix,
            (shape((rows, heads * DV), BF16), shape((rows, features), BF16)),
            (gain_out, w_mix[index], received, gates),
            2 * rows * features * heads * DV,
            "mix",
        )
        hidden, gate, up, active, part, *hidden_halves = local(
            ffn,
            (
                shape((rows, features), F32),
                shape((rows, hidden_width), F32),
                shape((rows, hidden_width), F32),
                shape((rows, hidden_width), BF16),
                shape((rows, features), BF16),
                *halves,
            ),
            (flag, gain_ffn, w_hidden[index], w_back[index], source, *sum_heads(part)),
            6 * rows * features * hidden_width,
            "ffn",
        )
        kept = dict(
            source=source,
            normed_halves=normed_halves,
            mixed=mixed,
            solves=solves,
            received=received,
            gates=gates,
            gated=gated,
            hidden=hidden,
            hidden_halves=hidden_halves,
            gate=gate,
            up=up,
            active=active,
            normed_all=lax.all_gather(after(normed, gated), "seq", axis=0, tiled=True),
        )
        return (hidden, *sum_heads(part)), kept

    def ffn_grad(flag_now, w_hidden_now, w_back_now, up_low, gate, up):
        grad_active = dot(up_low, w_back_now, NT)
        grad_gate = (grad_active * up * silu_grad(gate)).astype(BF16)
        grad_up = (grad_active * silu(gate)).astype(BF16)
        part = dot(grad_gate, w_hidden_now[:hidden_width]) + dot(grad_up, w_hidden_now[hidden_width:])
        return grad_gate, grad_up, part.astype(BF16), *by_core(flag_now, up_low)

    def mix_grad(flag_now, gain, gain_out, w_mix_now, upstream, hidden, one, two, received, gates):
        grad_hidden_norm = (one.astype(F32) + two.astype(F32)).astype(BF16).astype(F32)
        grad_hidden, grad_gain = norm_back(hidden, norm_scale(hidden, EPS), gain, grad_hidden_norm)
        grad_stream = upstream.astype(F32) + grad_hidden
        stream_low = grad_stream.astype(BF16)
        grad_gated = dot(stream_low, w_mix_now, NT)
        sent, grad_gates, grad_gain_out = [], [], 0.0
        for h in range(heads):
            out, gate_pre = outs_of(received, h), gates[:, h * DV : (h + 1) * DV]
            g = grad_gated[:, h * DV : (h + 1) * DV]
            scale = norm_scale(out, HEAD_EPS)
            grad_gates.append((g * out * scale * gain_out * silu_grad(gate_pre)).astype(BF16))
            grad_out, grad_one = norm_back(out, scale, gain_out, g * silu(gate_pre))
            grad_gain_out = grad_gain_out + grad_one
            for j in range(splits):
                sent.append(grad_out[:, j * width : (j + 1) * width].astype(BF16))
        return (
            grad_stream,
            jnp.stack(sent),
            jnp.concatenate(grad_gates, axis=1),
            grad_gain,
            grad_gain_out,
            *by_core(flag_now, grad_stream),
        )

    def front_grad(w_proj, w_rate_now, returned, grad_gates, grad_gain_out):
        part = 0.0
        lane = lax.broadcasted_iota(jnp.int32, (rows, 16), 1)
        grad_rates = jnp.zeros((rows, 16), F32)
        for h in range(heads):
            mine = [returned[h * splits + j].astype(F32) for j in range(splits)]
            total = sum(mine[1:], mine[0])
            pieces = [total[:, : 2 * DK].astype(BF16)]
            pieces += [m[:, 2 * DK : first_rate].astype(BF16) for m in mine]
            pieces.append(grad_gates[:, h * DV : (h + 1) * DV])
            grad = jnp.concatenate(pieces, axis=1)
            part = part + dot(grad, w_proj[:, h * columns : (h + 1) * columns], NT)
            r = first_rate
            grad_rates = jnp.where(lane == h, total[:, r : r + 1] + total[:, r + 1 : r + 2], grad_rates)
            grad_rates = jnp.where(
                lane == heads + h, total[:, r + 2 : r + 3] + total[:, r + 3 : r + 4], grad_rates
            )
        part = part + dot(grad_rates.astype(BF16), w_rate_now)
        extra = jnp.concatenate([grad_gain_out, jnp.zeros((1, features - DV), F32)], axis=1)
        extra = jnp.concatenate([extra, jnp.zeros((15, features), F32)], axis=0)
        return (jnp.concatenate([part, extra], axis=0).astype(BF16),)

    def source_grad(gain, source_low, grad_stream, one, two):
        summed = one.astype(F32) + two.astype(F32)
        source = source_low.astype(F32)
        grad_normed = summed[:rows].astype(BF16).astype(F32)
        grad_source, grad_gain = norm_back(source, norm_scale(source, EPS), gain, grad_normed)
        return (grad_stream + grad_source).astype(BF16), grad_gain, summed[rows : rows + 1, :DV]

    def weight_grads(groups):
        operands, widths = [], []
        for lefts, (mine, others) in groups:
            operands += [mine, swap_section(others)]
            for left in lefts:
                operands += [left, swap_section(left)]
            widths.append([left.shape[1] for left in lefts])

        def products(*values):
            values = list(values)
            out = []
            for sizes in widths:
                right, right_other = values.pop(0), values.pop(0)
                for _ in sizes:
                    out.append(
                        (dot(values.pop(0), right, TN) + dot(values.pop(0), right_other, TN)).astype(BF16)
                    )
            whole = jnp.concatenate(out, axis=0)
            return (jnp.stack([whole[:, p * half : (p + 1) * half] for p in range(parts)]),)

        total = sum(sum(sizes) for sizes in widths)
        return local(
            products,
            (shape((parts, total, half), BF16),),
            operands,
            4 * rows * total * parts * half,
            "weight_grads",
        )[0]

    def scatter_sum(whole):
        return lax.psum_scatter(whole, "seq", scatter_dimension=0, tiled=False)

    def backward(index, up_low, kept, earlier=None):
        gain_mix, gain_ffn, gain_out, params = smalls[index]
        grad_gate, grad_up, part, *up_halves = local(
            ffn_grad,
            (
                shape((rows, hidden_width), BF16),
                shape((rows, hidden_width), BF16),
                shape((rows, features), BF16),
                *halves,
            ),
            (flag, w_hidden[index], w_back[index], up_low, kept["gate"], kept["up"]),
            6 * rows * features * hidden_width,
            "ffn_grad",
        )
        one, two = sum_heads(part)
        ffn_whole = weight_grads(
            [([grad_gate, grad_up], kept["hidden_halves"]), ([kept["active"]], up_halves)]
        )
        one, ffn_whole = lax.optimization_barrier((one, ffn_whole))
        ffn_sums = scatter_sum(ffn_whole)
        grad_stream, sent, grad_gates, grad_gain_ffn, grad_gain_out, *stream_halves = local(
            mix_grad,
            (
                shape((rows, features), F32),
                shape((parts, rows, width), BF16),
                shape((rows, heads * DV), BF16),
                shape((1, features), F32),
                shape((1, DV), F32),
                *halves,
            ),
            (
                flag,
                gain_ffn,
                gain_out,
                w_mix[index],
                up_low,
                kept["hidden"],
                one,
                two,
                kept["received"],
                kept["gates"],
            ),
            2 * rows * features * heads * DV,
            "mix_grad",
        )
        grad_all = exchange_seq(sent).reshape(parts * rows, width)
        mix_whole = weight_grads([([kept["gated"]], stream_halves), ([grad_gates], kept["normed_halves"])])
        grad_all, mix_whole = lax.optimization_barrier((grad_all, mix_whole))
        if earlier is not None:
            grad_all, earlier_mix = lax.optimization_barrier((grad_all, earlier[1]))
            earlier = (earlier[0], earlier_mix) + earlier[2:]
        mix_sums = scatter_sum(mix_whole)
        grad_mixed, grad_params = local(
            lambda m, p, x, g: recur_backward(m, p, x, g, width),
            (shape((parts * rows, wide), BF16), shape((KW + 4, wide), F32)),
            (kept["mixed"], params, kept["solves"], grad_all),
            40 * 2 * parts * rows * DK * DK,
            "recur_backward",
            28 if parts * rows <= 512 else 60,
        )
        returned = exchange_seq(grad_mixed.reshape(parts, rows, wide))
        if earlier is not None:
            returned, ffn_sums = lax.optimization_barrier((returned, ffn_sums))
        (part,) = local(
            front_grad,
            (shape((rows + 16, features), BF16),),
            (w_project[index], w_rate[index], returned, grad_gates, grad_gain_out),
            2 * rows * features * heads * columns,
            "front_grad",
        )
        one, two = sum_heads(part)
        grad_input, grad_gain_mix, grad_gain_out = local(
            source_grad,
            (shape((rows, features), BF16), shape((1, features), F32), shape((1, DV), F32)),
            (gain_mix, kept["source"], grad_stream, one, two),
            10 * rows * features,
            "source_grad",
        )
        product = dot(kept["normed_all"], grad_mixed, TN).reshape(parts, 2, half, wide)
        mine = jnp.where(core == 0, product[:, 0], product[:, 1])
        others = jnp.where(core == 0, product[:, 1], product[:, 0])
        mine = (mine + swap_section(others.astype(BF16)).astype(F32)).astype(BF16)
        project_sums = exchange_seq(mine)
        grad_input, project_sums = lax.optimization_barrier((grad_input, project_sums))
        taps = jnp.zeros((KW, heads, qkv), F32)
        taps = lax.dynamic_update_slice(taps, grad_params[:KW, None, : 2 * DK], (0, own_head, 0))
        taps = lax.dynamic_update_slice(
            taps,
            grad_params[:KW, None, 2 * DK : first_rate],
            (0, own_head, 2 * DK + own_split * width),
        )
        one = jnp.arange(heads) == own_head
        logs = jnp.where(one, grad_params[KW, 0], 0.0)
        biases = jnp.where(one, grad_params[KW + 1, 0], 0.0)
        logs = jnp.concatenate([grad_gain_out[0], logs, biases])
        small = jnp.concatenate(
            [
                grad_gain_mix,
                grad_gain_ffn,
                taps.reshape(KW, heads * qkv),
                jnp.pad(logs, (0, features - DV - 2 * heads)).reshape(1, features),
                jnp.zeros((1, features), F32),
            ],
            axis=0,
        )
        return grad_input, (ffn_sums, mix_sums, project_sums, small), earlier

    pick = lambda a: jnp.where(core == 0, a[0], a[1])
    addends, kept_first = forward(0, (pick(inputs),))
    addends, kept_final = forward(1, addends)
    first = kept_final["source"]
    final = (addends[0] + (addends[1].astype(F32) + addends[2].astype(F32))).astype(BF16)
    grad_first, sums_final, _ = backward(1, pick(cotangent), kept_final)
    grad_first, ffn_final = lax.optimization_barrier((grad_first, sums_final[0]))
    sums_final = (ffn_final,) + sums_final[1:]
    grad_inputs, sums_first, sums_final = backward(0, grad_first, kept_first, sums_final)

    def settle(a_first, a_final):
        mine = jnp.where(core == 0, a_first, a_final)
        others = jnp.where(core == 0, a_final, a_first)
        return mine, swap_section(others)

    def ordered(flag_now, mine, others):
        mine, others = mine.astype(F32), others.astype(F32)
        first = jnp.broadcast_to(flag_now[:, :1], mine.shape) > 0.5
        return jnp.where(first, mine, others), jnp.where(first, others, mine)

    def join_ffn(flag_now, mine, others):
        whole = jnp.concatenate(ordered(flag_now, mine, others), axis=1)
        return whole[: 2 * hidden_width], whole[2 * hidden_width :]

    def join_project(flag_now, mix_mine, mix_others, mine, others):
        whole = jnp.concatenate(ordered(flag_now, mix_mine, mix_others), axis=1)
        gate_columns = whole[heads * DV :].T
        pieces, rates = [], []
        for h in range(heads):
            at = h * splits
            pair = [
                jnp.concatenate(ordered(flag_now, mine[at + j], others[at + j]), axis=0)
                for j in range(splits)
            ]
            total = sum(pair[1:], pair[0])
            pieces.append(total[:, : 2 * DK])
            pieces += [p[:, 2 * DK : first_rate] for p in pair]
            pieces.append(gate_columns[:, h * DV : (h + 1) * DV])
            rates.append(total[:, first_rate : first_rate + 4])
        lane = lax.broadcasted_iota(jnp.int32, (slab, LANES), 1)
        rate = jnp.zeros((slab, LANES), F32)
        for h in range(heads):
            rate = jnp.where(lane == h, rates[h][:, 0:1] + rates[h][:, 1:2], rate)
            rate = jnp.where(lane == heads + h, rates[h][:, 2:3] + rates[h][:, 3:4], rate)
        return whole[: heads * DV], jnp.concatenate(pieces, axis=1), rate

    grad_hidden_w, grad_back_w = local(
        join_ffn,
        (shape((2 * hidden_width, slab), F32), shape((hidden_width, slab), F32)),
        (flag, *settle(sums_first[0], sums_final[0])),
        1000000,
        "join_ffn",
    )
    grad_mix_w, grad_project_w, rate = local(
        join_project,
        (
            shape((heads * DV, slab), F32),
            shape((slab, heads * columns), F32),
            shape((slab, LANES), F32),
        ),
        (flag, *settle(sums_first[1], sums_final[1]), *settle(sums_first[2], sums_final[2])),
        1000000,
        "join_project",
    )
    small_mine, small_others = settle(sums_first[3], sums_final[3])
    small = sum_seq(small_mine + small_others)

    grad_hidden_w = jnp.transpose(grad_hidden_w.reshape(2, hidden_width, slab), (2, 0, 1))
    grad_mix_w = grad_mix_w.reshape(heads, DV, slab)
    grad_project_w = grad_project_w.reshape(slab, heads, columns)
    grad_rate_w = jnp.transpose(rate[:, : 2 * heads].reshape(slab, 2, heads), (1, 0, 2))
    grad_taps = small[2 : KW + 2].reshape(KW, heads, qkv)
    logs = small[KW + 2]

    def both(first_rows, final_rows):
        mine = jnp.where(core == 0, first_rows, final_rows)
        others = swap_section(jnp.where(core == 0, final_rows, first_rows))
        lead = jnp.where(core == 0, mine, others)
        follow = jnp.where(core == 0, others, mine)
        return jnp.stack([lead, follow])

    block_out = both(first, final)
    input_grad = both(grad_inputs, grad_first)
    return (
        block_out[None],
        input_grad[None],
        small[None, :2],
        grad_project_w[None],
        grad_rate_w[None],
        logs[None, DV : DV + heads],
        logs[None, DV + heads : DV + 2 * heads],
        grad_taps[None],
        logs[None, :DV],
        grad_mix_w[None],
        grad_hidden_w[None],
        grad_back_w[None],
    )


def solution(mesh):
    placed = (
        P(None, "seq", None),
        P(None, "seq", None),
        P("section", None, None),
        P("section", None, "head", None),
        P("section", None, None, "head"),
        P("section", "head"),
        P("section", "head"),
        P("section", None, "head", None),
        P("section", None),
        P("section", "head", None, None),
        P("section", None, None, "head"),
        P("section", "head", None),
    )
    return jax.shard_map(
        body,
        mesh=mesh,
        in_specs=placed,
        out_specs=(
            P("section", None, "seq", None),
            P("section", None, "seq", None),
            P("section", None, None),
            P("section", "seq", "head", None),
            P("section", None, "seq", "head"),
            P("section", "head"),
            P("section", "head"),
            P("section", None, "head", None),
            P("section", None),
            P("section", "head", None, "seq"),
            P("section", "seq", None, "head"),
            P("section", "head", "seq"),
        ),
        check_vma=False,
    )
```

```python
import functools
import math

import jax
import jax.numpy as jnp
from jax import lax
from jax.experimental import pallas as pl
from jax.experimental.pallas import tpu as pltpu
from jax.sharding import PartitionSpec as P

DK = 128
DV = 256
KW = 4
CHUNK = 128
LANES = 128
EPS = 1e-06
HEAD_EPS = 0.01
AXES = ("section", "seq", "head")
F32 = jnp.float32
BF16 = jnp.bfloat16


def route(move):
    sections, seqs, heads = (lax.axis_size(axis) for axis in AXES)
    pairs = []
    for s in range(sections):
        for z in range(seqs):
            for h in range(heads):
                s2, z2, h2 = move(s, z, h)
                pairs.append(((s * seqs + z) * heads + h, (s2 * seqs + z2) * heads + h2))
    return pairs


def swap_section(value):
    return lax.ppermute(value, AXES, route(lambda s, z, h: (1 - s, z, h)))


def sum_heads(part):
    return [part] + [
        lax.ppermute(part, AXES, route(lambda s, z, h: (s, z, h ^ k)))
        for k in range(1, lax.axis_size("head"))
    ]


def add_up(parts):
    parts = [part.astype(F32) for part in parts]
    while len(parts) > 1:
        parts = [a + b for a, b in zip(parts[::2], parts[1::2])]
    return parts[0]


def after(value, *first):
    return lax.optimization_barrier((value,) + first)[0]


def exchange_seq(value):
    return lax.all_to_all(value, "seq", 0, 0, tiled=False)


NN = (((1,), (0,)), ((), ()))
NT = (((1,), (1,)), ((), ()))
TN = (((0,), (0,)), ((), ()))


def raw(a, b, dims, passes):
    a_hi, b_hi = a.astype(BF16), b.astype(BF16)
    out = lax.dot_general(a_hi, b_hi, dims, preferred_element_type=F32)
    if passes > 1:
        a_lo = (a - a_hi.astype(F32)).astype(BF16)
        b_lo = (b - b_hi.astype(F32)).astype(BF16)
        out = out + lax.dot_general(a_hi, b_lo, dims, preferred_element_type=F32)
        out = out + lax.dot_general(a_lo, b_hi, dims, preferred_element_type=F32)
    return out


@functools.partial(jax.custom_vjp, nondiff_argnums=(2,))
def nn(a, b, passes=1):
    return raw(a, b, NN, passes)


nn.defvjp(
    lambda a, b, p: (raw(a, b, NN, p), (a, b)),
    lambda p, kept, g: (raw(g, kept[1], NT, p), raw(kept[0], g, TN, p)),
)


@functools.partial(jax.custom_vjp, nondiff_argnums=(2,))
def nt(a, b, passes=1):
    return raw(a, b, NT, passes)


nt.defvjp(
    lambda a, b, p: (raw(a, b, NT, p), (a, b)),
    lambda p, kept, g: (raw(g, kept[1], NN, p), raw(g, kept[0], TN, p)),
)


@functools.partial(jax.custom_vjp, nondiff_argnums=(2,))
def tn(a, b, passes=1):
    return raw(a, b, TN, passes)


tn.defvjp(
    lambda a, b, p: (raw(a, b, TN, p), (a, b)),
    lambda p, kept, g: (raw(kept[1], g, NT, p), raw(kept[0], g, NN, p)),
)


def lower_ones():
    rows = lax.broadcasted_iota(jnp.int32, (CHUNK, CHUNK), 0)
    columns = lax.broadcasted_iota(jnp.int32, (CHUNK, CHUNK), 1)
    return jnp.where(rows >= columns, 1.0, 0.0)


def split3(v):
    hi = v.astype(BF16)
    rest = v - hi.astype(F32)
    mid = rest.astype(BF16)
    return hi, mid, (rest - mid.astype(F32)).astype(BF16)


@jax.custom_vjp
def running(v):
    ones = lower_ones().astype(BF16)
    return sum(lax.dot_general(ones, piece, NN, preferred_element_type=F32) for piece in split3(v))


def running_back(kept, g):
    ones = lower_ones().astype(BF16)
    return (sum(lax.dot_general(ones, piece, TN, preferred_element_type=F32) for piece in split3(g)),)


running.defvjp(lambda v: (running(v), None), running_back)


def inverse_value(lowers):
    rows = lax.broadcasted_iota(jnp.int32, (CHUNK, CHUNK), 0)
    columns = lax.broadcasted_iota(jnp.int32, (CHUNK, CHUNK), 1)
    results = [jnp.where(rows == columns, 1.0, 0.0)] * len(lowers)
    size = 1
    while size < CHUNK:
        joined = (rows // (2 * size) == columns // (2 * size)) & (rows // size != columns // size)
        between = [jnp.where(joined, lower, 0.0) for lower in lowers]
        if size == 1:
            results = [r - b for r, b in zip(results, between)]
        else:
            middle = [raw(b, r, NN, 3) for r, b in zip(results, between)]
            results = [r - raw(r, m, NN, 3) for r, m in zip(results, middle)]
        size *= 2
    return tuple(results)


@jax.custom_vjp
def inverse(lowers, values):
    return inverse_value(lowers) if values is None else values


def inverse_keep(lowers, values):
    values = inverse(lowers, values)
    return values, values


def inverse_back(values, grads):
    first = [raw(value, g, TN, 1) for value, g in zip(values, grads)]
    return tuple(-raw(f, value, NT, 1) for f, value in zip(first, values)), None


inverse.defvjp(inverse_keep, inverse_back)


def roll_rows(v, distance):
    return pltpu.roll(v, distance, 0)


@functools.partial(jax.custom_vjp, nondiff_argnums=(1,))
def shift_rows(v, distance):
    rows = lax.broadcasted_iota(jnp.int32, v.shape, 0)
    return jnp.where(rows >= distance, roll_rows(v, distance), 0.0)


def shift_back(distance, kept, g):
    rows = lax.broadcasted_iota(jnp.int32, g.shape, 0)
    return (jnp.where(rows < g.shape[0] - distance, roll_rows(g, g.shape[0] - distance), 0.0),)


shift_rows.defvjp(lambda v, d: (shift_rows(v, d), None), shift_back)


@jax.custom_vjp
def split_rows(v):
    return tuple(v[i : i + CHUNK] for i in range(0, v.shape[0], CHUNK))


split_rows.defvjp(lambda v: (split_rows(v), None), lambda kept, g: (jnp.concatenate(g, axis=0),))


@jax.custom_vjp
def low(v):
    return v.astype(BF16).astype(F32)


low.defvjp(lambda v: (low(v), None), lambda kept, g: (g,))


@jax.custom_vjp
def softplus(v):
    return jnp.maximum(v, 0.0) + jnp.log1p(jnp.exp(-jnp.abs(v)))


softplus.defvjp(lambda v: (softplus(v), v), lambda v, g: (g * jax.nn.sigmoid(v),))


def silu(v):
    return v * jax.nn.sigmoid(v)


def unit_norm(v):
    return v * lax.rsqrt(jnp.sum(v * v, axis=-1, keepdims=True) + EPS)


def convolve(rows_in, taps):
    total = taps[KW - 1] * rows_in
    for j in range(KW - 1):
        total = total + taps[j] * shift_rows(rows_in, KW - 1 - j)
    return total


def to_column(row):
    wide = jnp.broadcast_to(row, (CHUNK, CHUNK))
    rows = lax.broadcasted_iota(jnp.int32, wide.shape, 0)
    columns = lax.broadcasted_iota(jnp.int32, wide.shape, 1)
    return jnp.sum(jnp.where(rows == columns, wide, 0.0), axis=1, keepdims=True)


def recurrence(
    x_q, x_k, x_v, decay_raw, strength_raw, taps_q, taps_k, taps_v, decay_log, decay_bias, solves=None
):
    queries = low(unit_norm(silu(convolve(x_q, taps_q))) * DK**-0.5)
    keys = low(unit_norm(silu(convolve(x_k, taps_k))))
    values = low(silu(convolve(x_v, taps_v)))
    strength = [to_column(jax.nn.sigmoid(row)) for row in strength_raw]
    decay_rows = [-jnp.exp(decay_log) * softplus(row + decay_bias) for row in decay_raw]
    log_decay = [to_column(row) for row in decay_rows]
    rows = lax.broadcasted_iota(jnp.int32, (CHUNK, CHUNK), 0)
    columns = lax.broadcasted_iota(jnp.int32, (CHUNK, CHUNK), 1)
    queries, keys, values = (split_rows(a) for a in (queries, keys, values))
    chunks = range(len(keys))
    totals = [running(jnp.broadcast_to(ld, (CHUNK, CHUNK))) for ld in log_decay]
    wholes = [jnp.sum(row, axis=1, keepdims=True) for row in decay_rows]
    within = []
    for total in totals:
        spread = total - total.T
        within.append(
            jnp.where(rows >= columns, jnp.exp(jnp.where(rows >= columns, spread, 0.0)), 0.0)
        )
    grown = [jnp.exp(total) for total in totals]
    weighted = [strength[i] * keys[i] for i in chunks]
    lowers = tuple(
        strength[i] * nt(keys[i], keys[i]) * jnp.where(rows > columns, within[i], 0.0)
        for i in chunks
    )
    solve = inverse(lowers, solves)
    part_v = [nn(solve[i], strength[i] * values[i]) for i in chunks]
    part_k = [nn(solve[i], weighted[i] * grown[i]) for i in chunks]
    scores = [nt(queries[i], keys[i]) * within[i] for i in chunks]
    ending = [keys[i] * jnp.exp(wholes[i] - totals[i]) for i in chunks]
    seen = [queries[i] * grown[i] - nn(scores[i], part_k[i]) for i in chunks]
    own = [nn(scores[i], part_v[i]) for i in chunks]
    forget = [tn(ending[i], part_k[i]) for i in chunks]
    learn = [tn(ending[i], part_v[i]) for i in chunks]
    state = jnp.zeros((DK, x_v.shape[1]), F32)
    out = []
    for i in chunks:
        out.append(nn(seen[i], state) + own[i])
        state = jnp.exp(wholes[i]) * state + learn[i] - nn(forget[i], state)
    return jnp.concatenate(out, axis=0), solve


def with_rates(channels, decay_row, strength_row):
    rows = []
    for row in (decay_row, strength_row):
        hi = row.astype(BF16).astype(F32)
        rows += [hi, row - hi]
    rows = jnp.concatenate(rows + [jnp.zeros((12, row.shape[1]), F32)], axis=0)
    missing = channels.shape[1] - rows.shape[1]
    rows = jnp.concatenate([rows, jnp.zeros((16, missing), F32)], axis=1)
    return jnp.concatenate([channels, rows], axis=0).astype(BF16)


def rates_of(rows, count):
    rows = rows.astype(F32)
    return rows[0:1, :count] + rows[1:2, :count], rows[2:3, :count] + rows[3:4, :count]


def unpack(mixed, params, width):
    chunks = mixed.shape[0]
    x = mixed[:, :CHUNK].reshape(chunks * CHUNK, mixed.shape[2]).astype(F32)
    rates = [rates_of(mixed[i, CHUNK:], CHUNK) for i in range(chunks)]
    taps_q = [params[j : j + 1, :DK] for j in range(KW)]
    taps_k = [params[j : j + 1, DK : 2 * DK] for j in range(KW)]
    taps_v = [params[j : j + 1, 2 * DK : 2 * DK + width] for j in range(KW)]
    return (
        x[:, :DK],
        x[:, DK : 2 * DK],
        x[:, 2 * DK :],
        [r[0] for r in rates],
        [r[1] for r in rates],
        taps_q,
        taps_k,
        taps_v,
        params[KW : KW + 1, 0:1],
        params[KW + 1 : KW + 2, 0:1],
    )


def recur_forward(mixed, params, width):
    out, solve = recurrence(*unpack(mixed, params, width))
    return out.astype(BF16), jnp.concatenate(solve, axis=0).astype(BF16)


def recur_backward(mixed, params, solves, grad_out, width):
    solves = tuple(v.astype(F32) for v in split_rows(solves))
    unused, back = jax.vjp(
        lambda *a: recurrence(*a, solves=solves)[0], *unpack(mixed, params, width)
    )
    g_q, g_k, g_v, g_decay, g_strength, g_tq, g_tk, g_tv, g_log, g_bias = back(grad_out.astype(F32))
    wide = mixed.shape[2]
    channels = jnp.concatenate([g_q, g_k, g_v], axis=1)
    grad_mixed = jnp.stack(
        [with_rates(c, d, g) for c, d, g in zip(split_rows(channels), g_decay, g_strength)]
    )
    rows = [jnp.concatenate([g_tq[j], g_tk[j], g_tv[j]], axis=1) for j in range(KW)]
    rows.append(jnp.broadcast_to(g_log, (1, wide)))
    rows.append(jnp.broadcast_to(g_bias, (1, wide)))
    rows.append(jnp.zeros((2, wide), F32))
    return grad_mixed, jnp.concatenate(rows, axis=0)


def dot(a, b, dims=NN):
    return lax.dot_general(a, b, dims, preferred_element_type=F32)


def norm_scale(v, eps):
    return lax.rsqrt(jnp.mean(v * v, axis=-1, keepdims=True) + eps)


def norm_back(v, scale, gain, grad):
    gained = gain * grad
    mean = jnp.mean(gained * v, axis=-1, keepdims=True)
    grad_v = scale * gained - v * (scale * scale * scale) * mean
    return grad_v, jnp.sum(grad * v * scale, axis=0, keepdims=True)


def silu_grad(v):
    s = jax.nn.sigmoid(v)
    return s * (1.0 + v * (1.0 - s))


class Fetched:
    def __init__(self, slot, copies, step):
        self.slot, self.copies, self.step = slot, copies, step

    def wait(self, first, last):
        for i in range(first, last):
            if self.copies[i] is not None:
                self.copies[i].wait()
                self.copies[i] = None

    def __call__(self):
        self.wait(0, len(self.copies))
        return self.slot[...]

    def rows(self, low_row, high_row):
        self.wait(low_row // self.step, -(-high_row // self.step))
        return self.slot[low_row:high_row]


def pieces_of(array):
    large = math.prod(array.shape) * array.dtype.itemsize > 1000000
    return 4 if large and len(array.shape) == 2 and array.shape[0] % 64 == 0 else 1


def local(function, shapes, operands, flops, name, choice=None):
    pairs = [op if isinstance(op, (tuple, list)) else (op,) for op in operands]
    flat = [a for pair in pairs for a in pair]
    outs = len(shapes)
    chosen = any(len(pair) > 1 for pair in pairs)

    def kernel(*refs):
        refs = list(refs)
        flag = refs.pop(0) if chosen else None
        sources = [[refs.pop(0) for _ in pair] for pair in pairs]
        results = [refs.pop(0) for _ in shapes]
        slots = [refs.pop(0) for _ in pairs]
        stages = [refs.pop(0) for _ in shapes]
        in_sem, out_sem = refs
        fetched, used = [], 0
        for choices, slot in zip(sources, slots):
            number = pieces_of(slot)
            step = slot.shape[0] // number
            waits = []
            for i in range(number):
                cut = (lambda r: r) if number == 1 else (lambda r: r.at[pl.ds(i * step, step)])
                copies = [pltpu.make_async_copy(cut(c), cut(slot), in_sem.at[used]) for c in choices]
                used += 1
                if len(copies) == 1:
                    copies[0].start()
                else:
                    pl.when(flag[0] == 1)(copies[0].start)
                    pl.when(flag[0] != 1)(copies[1].start)
                waits.append(copies[0])
            fetched.append(Fetched(slot, waits, step))
        leaving = []
        for i, value in enumerate(function(*fetched)):
            stages[i][...] = value
            leaving.append(pltpu.make_async_copy(stages[i], results[i], out_sem.at[i]))
            leaving[-1].start()
        for one in fetched:
            one.wait(0, len(one.copies))
        for copy in leaving:
            copy.wait()

    moved = sum(math.prod(a.shape) * a.dtype.itemsize for a in ([p[0] for p in pairs] + list(shapes)))
    far = pl.BlockSpec(memory_space=pltpu.HBM)
    return pl.pallas_call(
        kernel,
        out_shape=tuple(shapes),
        in_specs=[pl.BlockSpec(memory_space=pltpu.SMEM)] * chosen + [far] * len(flat),
        out_specs=(far,) * outs,
        scratch_shapes=[pltpu.VMEM(p[0].shape, p[0].dtype) for p in pairs]
        + [pltpu.VMEM(a.shape, a.dtype) for a in shapes]
        + [pltpu.SemaphoreType.DMA((sum(pieces_of(p[0]) for p in pairs),)), pltpu.SemaphoreType.DMA((outs,))],
        compiler_params=pltpu.CompilerParams(vmem_limit_bytes=60 * 1024 * 1024),
        cost_estimate=pl.CostEstimate(flops=flops, bytes_accessed=moved, transcendentals=0),
        name=name,
    )(*([choice] * chosen), *flat)


def body(
    inputs,
    cotangent,
    gains,
    w_in,
    w_rates,
    a_log,
    dt_bias,
    conv_kernel,
    out_gain,
    w_out,
    w_ffn_in,
    w_down,
):
    core = lax.axis_index("section")
    place = lax.axis_index("seq")
    parts = lax.axis_size("seq")
    micro, rows, features = inputs.shape
    heads = w_in.shape[2]
    columns = w_in.shape[3]
    qkv = 2 * DK + DV
    hidden_width = w_ffn_in.shape[3]
    splits = parts // heads
    width = DV // splits
    wide = 2 * DK + width
    tall = rows + 16
    own_head = place // splits
    own_split = place % splits
    slab = features // parts
    half = slab // 2
    shape = jax.ShapeDtypeStruct

    def pair(own):
        return own, swap_section(own)

    own_first = (core == 0).astype(jnp.int32).reshape(1)
    choices = (own_first, 1 - own_first)
    w_project = pair(w_in[0].reshape(features, heads * columns))
    rate_rows = jnp.transpose(w_rates[0], (0, 2, 1)).reshape(2 * heads, features)
    w_rate = pair(jnp.pad(rate_rows, ((0, 16 - 2 * heads), (0, 0))))
    logs = jnp.concatenate([out_gain[0], a_log[0], dt_bias[0]])
    flats = pair(
        jnp.concatenate(
            [
                gains[0],
                conv_kernel[0].reshape(KW, heads * qkv),
                jnp.pad(logs, (0, features - DV - 2 * heads)).reshape(1, features),
                jnp.zeros((1, features), F32),
            ],
            axis=0,
        )
    )
    w_mix = pair(w_out[0].reshape(heads * DV, features))
    w_hidden = pair(jnp.transpose(w_ffn_in[0], (1, 2, 0)).reshape(2 * hidden_width, features))
    w_back = pair(w_down[0])
    inputs_own = jnp.where(core == 0, inputs[0], inputs[1])

    def small_params(index, held):
        flat = jnp.where(core == index, *held)
        logs = flat[KW + 2 : KW + 3]
        taps = flat[2 : KW + 2].reshape(KW, heads, qkv)
        taps = lax.dynamic_index_in_dim(taps, own_head, 1, keepdims=False)
        taps_v = lax.dynamic_slice_in_dim(taps, 2 * DK + own_split * width, width, 1)
        log = lax.dynamic_index_in_dim(logs[0, DV : DV + heads], own_head, 0, keepdims=False)
        bias = lax.dynamic_index_in_dim(
            logs[0, DV + heads : DV + 2 * heads], own_head, 0, keepdims=False
        )
        params = jnp.concatenate(
            [
                jnp.concatenate([taps[:, : 2 * DK], taps_v], axis=1),
                jnp.full((1, wide), log),
                jnp.full((1, wide), bias),
                jnp.zeros((2, wide), F32),
            ],
            axis=0,
        )
        return flat[0:1], flat[1:2], logs[:, :DV], params

    smalls = [(jnp.where(core == 0, flats[0][0:1], flats[1][0:1]),), None]

    flag = jnp.broadcast_to(jnp.where(core == 0, 1.0, 0.0).astype(F32), (1, LANES))

    def by_core(flag_now, value):
        first = jnp.broadcast_to(flag_now[:, :half], (value.shape[0], half)) > 0.5
        mine, others = [], []
        for p in range(parts):
            a = value[:, p * slab : p * slab + half].astype(F32)
            b = value[:, p * slab + half : (p + 1) * slab].astype(F32)
            mine.append(jnp.where(first, a, b))
            others.append(jnp.where(first, b, a))
        return [jnp.concatenate(v, axis=1).astype(BF16) for v in (mine, others)]

    def project_grad(flag_now, normed_all, grad_mixed):
        normed_all, grad_mixed = normed_all(), grad_mixed()
        channels = grad_mixed[:, :rows].reshape(parts * rows, wide)
        product = dot(normed_all, channels, TN)
        rates = jnp.concatenate([grad_mixed[p, rows:, :rows] for p in range(parts)], axis=1)
        rates = dot(rates, normed_all)
        decay, strength = rates[0:1] + rates[1:2], rates[2:3] + rates[3:4]
        mine, others = [], []
        for p in range(parts):
            cuts = []
            for c in range(2):
                at = p * slab + c * half
                cut = slice(at, at + half)
                cuts.append(with_rates(product[cut], decay[:, cut], strength[:, cut]).astype(F32))
            first = jnp.broadcast_to(flag_now()[:, :1], cuts[0].shape) > 0.5
            mine.append(jnp.where(first, cuts[0], cuts[1]).astype(BF16))
            others.append(jnp.where(first, cuts[1], cuts[0]).astype(BF16))
        yield jnp.stack(mine)
        yield jnp.stack(others)

    halves = (shape((rows, parts * half), BF16),) * 2

    def outs_of(received, h):
        return jnp.concatenate([received[h * splits + j] for j in range(splits)], axis=1).astype(F32)

    def front(flag_now, gain, w_rate_now, w_proj, *addends):
        source = addends[0]().astype(F32)
        if len(addends) > 1:
            source = source + add_up([a() for a in addends[1:]])
        source_low = source.astype(BF16)
        yield source_low
        source = source_low.astype(F32)
        normed = (source * norm_scale(source, EPS) * gain()).astype(BF16)
        yield normed
        yield from by_core(flag_now(), normed)
        rates = dot(w_rate_now(), normed, NT)
        quarter = features // 4
        whole = 0.0
        for i in range(4):
            at = i * quarter
            whole = whole + dot(normed[:, at : at + quarter], w_proj.rows(at, at + quarter))
        sent, gates = [], []
        for h in range(heads):
            projected = whole[:, h * columns : (h + 1) * columns]
            for j in range(splits):
                v_at = 2 * DK + j * width
                channels = [projected[:, : 2 * DK], projected[:, v_at : v_at + width]]
                sent.append(
                    with_rates(
                        jnp.concatenate(channels, axis=1),
                        rates[h : h + 1],
                        rates[heads + h : heads + h + 1],
                    )
                )
            gates.append(projected[:, qkv:])
        yield jnp.stack(sent)
        yield jnp.concatenate(gates, axis=1)

    def recur(params, mixed):
        yield from recur_forward(mixed(), params(), width)

    def mix(gain_out, gates, w_mix_now, received):
        gated = []
        received, gates = received(), gates()
        for h in range(heads):
            out = outs_of(received, h)
            gate = gates[:, h * DV : (h + 1) * DV]
            gated.append((out * norm_scale(out, HEAD_EPS) * gain_out() * silu(gate)).astype(BF16))
        gated = jnp.concatenate(gated, axis=1)
        yield dot(gated, w_mix_now()).astype(BF16)
        yield gated

    def ffn(flag_now, gain, source, one, two, three, four, w_hidden_now, w_back_now):
        hidden = source().astype(F32) + add_up([one(), two(), three(), four()])
        yield hidden
        hidden_norm = (hidden * norm_scale(hidden, EPS) * gain()).astype(BF16)
        yield from by_core(flag_now(), hidden_norm)
        gate = dot(hidden_norm, w_hidden_now.rows(0, hidden_width), NT)
        yield gate
        up = dot(hidden_norm, w_hidden_now.rows(hidden_width, 2 * hidden_width), NT)
        yield up
        active = (silu(gate) * up).astype(BF16)
        yield active
        yield dot(active, w_back_now()).astype(BF16)

    def forward(index, addends):
        gain_mix = smalls[index][0]
        source, normed, *normed_halves, sent, gates = local(
            front,
            (
                shape((rows, features), BF16),
                shape((rows, features), BF16),
                *halves,
                shape((parts, tall, wide), BF16),
                shape((rows, heads * DV), F32),
            ),
            (flag, gain_mix, w_rate, w_project, *addends),
            2 * rows * features * heads * columns,
            "front",
            choices[index],
        )
        mixed = exchange_seq(sent)
        if index == 0:
            held = lax.optimization_barrier((*flats, sent))[:2]
            smalls[:] = [small_params(0, held), small_params(1, held)]
        gain_mix, gain_ffn, gain_out, params = smalls[index]
        recurrent, solves = local(
            recur,
            (shape((parts * rows, width), BF16), shape((parts * rows, CHUNK), BF16)),
            (params, mixed),
            20 * 2 * parts * rows * DK * DK,
            "recur_forward",
        )
        received = exchange_seq(recurrent.reshape(parts, rows, width))
        part, gated = local(
            mix,
            (shape((rows, features), BF16), shape((rows, heads * DV), BF16)),
            (gain_out, gates, w_mix, received),
            2 * rows * features * heads * DV,
            "mix",
            choices[index],
        )
        summands = sum_heads(part)
        gate_shape = shape((rows, hidden_width), F32)
        active_shape = shape((rows, hidden_width), BF16)
        part_shape = shape((rows, features), BF16)
        extra = {}
        if index == 0:
            hidden, *hidden_halves, gate, up, active, part = local(
                ffn,
                (shape((rows, features), F32), *halves, gate_shape, gate_shape, active_shape, part_shape),
                (flag, gain_ffn, source, *summands, w_hidden, w_back),
                6 * rows * features * hidden_width,
                "ffn",
                choices[index],
            )
            extra = dict(gate=gate, up=up)
        else:
            up_low = jnp.where(core == 0, cotangent[0], cotangent[1])
            hidden, *both_halves, grad_gate, grad_up, part_grad, active, part = local(
                ffn_both,
                (
                    shape((rows, features), F32),
                    *halves,
                    *halves,
                    active_shape,
                    active_shape,
                    part_shape,
                    active_shape,
                    part_shape,
                ),
                (flag, gain_ffn, source, *summands, up_low, w_hidden, w_back),
                12 * rows * features * hidden_width,
                "ffn_both",
                choices[index],
            )
            hidden_halves = both_halves[:2]
            extra = dict(up_low=up_low, up_halves=both_halves[2:], part=part_grad)
            extra.update(grad_gate=grad_gate, grad_up=grad_up)
        kept = dict(
            source=source,
            normed_halves=normed_halves,
            mixed=mixed,
            solves=solves,
            received=received,
            gates=gates,
            gated=gated,
            hidden=hidden,
            hidden_halves=hidden_halves,
            active=active,
            **extra,
            normed_all=lax.all_gather(after(normed, gated), "seq", axis=0, tiled=True),
        )
        if index == 0:
            summands = sum_heads(part)
            summands, kept["normed_all"] = lax.optimization_barrier((summands, kept["normed_all"]))
            return (hidden, *summands), kept
        return (hidden, part), kept

    def ffn_grad(flag_now, up_low, w_back_now, gate, up, w_hidden_now):
        yield from by_core(flag_now(), up_low())
        grad_active = dot(up_low(), w_back_now(), NT)
        gate, up = gate(), up()
        grad_gate = (grad_active * up * silu_grad(gate)).astype(BF16)
        grad_up = (grad_active * silu(gate)).astype(BF16)
        part = dot(grad_gate, w_hidden_now.rows(0, hidden_width))
        part = part + dot(grad_up, w_hidden_now.rows(hidden_width, 2 * hidden_width))
        yield part.astype(BF16)
        yield grad_gate
        yield grad_up

    def ffn_both(flag_now, gain, source, one, two, three, four, up_low, w_hidden_now, w_back_now):
        hidden = source().astype(F32) + add_up([one(), two(), three(), four()])
        yield hidden
        hidden_norm = (hidden * norm_scale(hidden, EPS) * gain()).astype(BF16)
        yield from by_core(flag_now(), hidden_norm)
        yield from by_core(flag_now(), up_low())
        gate = dot(hidden_norm, w_hidden_now.rows(0, hidden_width), NT)
        up = dot(hidden_norm, w_hidden_now.rows(hidden_width, 2 * hidden_width), NT)
        grad_active = dot(up_low(), w_back_now(), NT)
        grad_gate = (grad_active * up * silu_grad(gate)).astype(BF16)
        yield grad_gate
        grad_up = (grad_active * silu(gate)).astype(BF16)
        yield grad_up
        part = dot(grad_gate, w_hidden_now.rows(0, hidden_width))
        part = part + dot(grad_up, w_hidden_now.rows(hidden_width, 2 * hidden_width))
        yield part.astype(BF16)
        active = (silu(gate) * up).astype(BF16)
        yield active
        yield dot(active, w_back_now()).astype(BF16)

    def source_ffn_grad(
        flag_now, gain, source_low, one, two, three, four, grad_stream, w_back_now, gate, up, w_hidden_now
    ):
        grad_input, *rest = source_grad(gain, source_low, grad_stream, one, two, three, four)
        yield grad_input
        yield from rest
        yield from ffn_grad(flag_now, lambda: grad_input, w_back_now, gate, up, w_hidden_now)

    def mix_grad(
        flag_now, gain, gain_out, hidden, upstream, one, two, three, four, w_mix_now, received, gates
    ):
        hidden = hidden()
        grad_hidden_norm = add_up([one(), two(), three(), four()]).astype(BF16).astype(F32)
        grad_hidden, grad_gain = norm_back(hidden, norm_scale(hidden, EPS), gain(), grad_hidden_norm)
        grad_stream = upstream().astype(F32) + grad_hidden
        yield grad_stream
        yield grad_gain
        yield from by_core(flag_now(), grad_stream)
        grad_gated = dot(grad_stream.astype(BF16), w_mix_now(), NT)
        received, gates = received(), gates()
        sent, grad_gates, grad_gain_out = [], [], 0.0
        for h in range(heads):
            out, gate_pre = outs_of(received, h), gates[:, h * DV : (h + 1) * DV]
            g = grad_gated[:, h * DV : (h + 1) * DV]
            scale = norm_scale(out, HEAD_EPS)
            grad_gates.append((g * out * scale * gain_out() * silu_grad(gate_pre)).astype(BF16))
            grad_out, grad_one = norm_back(out, scale, gain_out(), g * silu(gate_pre))
            grad_gain_out = grad_gain_out + grad_one
            for j in range(splits):
                sent.append(grad_out[:, j * width : (j + 1) * width].astype(BF16))
        yield jnp.stack(sent)
        yield jnp.concatenate(grad_gates, axis=1)
        yield grad_gain_out

    def recur_grad(params, mixed, solves, grad_out):
        yield from recur_backward(mixed(), params(), solves(), grad_out(), width)

    def front_grad(w_rate_now, grad_gates, grad_gain_out, returned, w_proj):
        grads = []
        grad_rates = [[], []]
        grad_gates, returned = grad_gates(), returned()
        for h in range(heads):
            mine = [returned[h * splits + j] for j in range(splits)]
            channels = [m[:rows].astype(F32) for m in mine]
            pieces = [sum((c[:, : 2 * DK] for c in channels[1:]), channels[0][:, : 2 * DK]).astype(BF16)]
            pieces += [m[:rows, 2 * DK :] for m in mine]
            pieces.append(grad_gates[:, h * DV : (h + 1) * DV])
            grads += pieces
            rates = [rates_of(m[rows:], rows) for m in mine]
            for r in range(2):
                grad_rates[r].append(sum((x[r] for x in rates[1:]), rates[0][r]))
        grad_rates = grad_rates[0] + grad_rates[1] + [jnp.zeros((16 - 2 * heads, rows), F32)]
        grad_rates = jnp.concatenate(grad_rates, axis=0).astype(BF16)
        part = dot(grad_rates, w_rate_now(), TN)
        grad = jnp.concatenate(grads, axis=1)
        quarter = features // 4
        cuts = [dot(grad, w_proj.rows(i * quarter, (i + 1) * quarter), NT) for i in range(4)]
        part = part + jnp.concatenate(cuts, axis=1)
        extra = jnp.concatenate([grad_gain_out(), jnp.zeros((1, features - DV), F32)], axis=1)
        extra = jnp.concatenate([extra, jnp.zeros((15, features), F32)], axis=0)
        yield jnp.concatenate([part, extra], axis=0).astype(BF16)

    def source_grad(gain, source_low, grad_stream, one, two, three, four):
        source = source_low().astype(F32)
        scale = norm_scale(source, EPS)
        summed = add_up([one(), two(), three(), four()])
        grad_normed = summed[:rows].astype(BF16).astype(F32)
        grad_source, grad_gain = norm_back(source, scale, gain(), grad_normed)
        yield (grad_stream() + grad_source).astype(BF16)
        yield grad_gain
        yield summed[rows : rows + 1, :DV]

    def weight_grads(groups):
        operands, counts, total = [], [], 0
        for lefts, (mine, others) in groups:
            operands += [mine, swap_section(others)]
            for left in lefts:
                operands += [left, swap_section(left)]
            counts.append(len(lefts))
            total += sum(left.shape[1] for left in lefts)

        def products(*values):
            values = list(values)
            out = []
            for count in counts:
                right, right_other = values.pop(0), values.pop(0)
                for _ in range(count):
                    left, left_other = values.pop(0), values.pop(0)
                    both = dot(left(), right(), TN) + dot(left_other(), right_other(), TN)
                    out.append(both.astype(BF16))
            whole = jnp.concatenate(out, axis=0)
            yield jnp.stack([whole[:, p * half : (p + 1) * half] for p in range(parts)])

        return local(
            products,
            (shape((parts, total, half), BF16),),
            operands,
            4 * rows * total * parts * half,
            "weight_grads",
        )[0]

    def scatter_sum(whole):
        return lax.psum_scatter(whole, "seq", scatter_dimension=0, tiled=False)

    active_shape = shape((rows, hidden_width), BF16)
    part_shape = shape((rows, features), BF16)

    def backward(index, kept, earlier=None, before=None):
        gain_mix, gain_ffn, gain_out, params = smalls[index]
        up_low = kept["up_low"]
        summands = sum_heads(kept["part"])
        ffn_whole = weight_grads(
            [
                ([kept["grad_gate"], kept["grad_up"]], kept["hidden_halves"]),
                ([kept["active"]], kept["up_halves"]),
            ]
        )
        summands, ffn_whole = lax.optimization_barrier((summands, ffn_whole))
        if earlier is None:
            summands, kept["normed_all"] = lax.optimization_barrier((summands, kept["normed_all"]))
        ffn_sums = scatter_sum(ffn_whole)
        grad_stream, grad_gain_ffn, *stream_halves, sent, grad_gates, grad_gain_out = local(
            mix_grad,
            (
                shape((rows, features), F32),
                shape((1, features), F32),
                *halves,
                shape((parts, rows, width), BF16),
                shape((rows, heads * DV), BF16),
                shape((1, DV), F32),
            ),
            (
                flag,
                gain_ffn,
                gain_out,
                kept["hidden"],
                up_low,
                *summands,
                w_mix,
                kept["received"],
                kept["gates"],
            ),
            2 * rows * features * heads * DV,
            "mix_grad",
            choices[index],
        )
        grad_all = exchange_seq(sent).reshape(parts * rows, width)
        mix_whole = weight_grads([([kept["gated"]], stream_halves), ([grad_gates], kept["normed_halves"])])
        grad_all, mix_whole = lax.optimization_barrier((grad_all, mix_whole))
        if earlier is not None:
            grad_all, *tied = lax.optimization_barrier((grad_all, *earlier[:2]))
            earlier = tuple(tied) + earlier[2:]
        mix_sums = scatter_sum(mix_whole)
        grad_mixed, grad_params = local(
            recur_grad,
            (shape((parts, tall, wide), BF16), shape((KW + 4, wide), F32)),
            (params, kept["mixed"], kept["solves"], grad_all),
            40 * 2 * parts * rows * DK * DK,
            "recur_backward",
        )
        returned = exchange_seq(grad_mixed)
        mine, others = local(
            project_grad,
            (shape((parts, half + 16, wide), BF16),) * 2,
            (flag, kept["normed_all"], grad_mixed),
            2 * parts * rows * features * wide,
            "project_grad",
        )
        mine = (mine.astype(F32) + swap_section(others).astype(F32)).astype(BF16)
        returned, mine = lax.optimization_barrier((returned, mine))
        project_sums = exchange_seq(mine)
        (part,) = local(
            front_grad,
            (shape((rows + 16, features), BF16),),
            (w_rate, grad_gates, grad_gain_out, returned, w_project),
            2 * rows * features * heads * columns,
            "front_grad",
            choices[index],
        )
        summands = sum_heads(part)
        taps = jnp.zeros((KW, heads, qkv), F32)
        taps = lax.dynamic_update_slice(taps, grad_params[:KW, None, : 2 * DK], (0, own_head, 0))
        taps = lax.dynamic_update_slice(
            taps,
            grad_params[:KW, None, 2 * DK :],
            (0, own_head, 2 * DK + own_split * width),
        )
        one = jnp.arange(heads) == own_head
        logs = jnp.where(one, grad_params[KW, 0], 0.0)
        biases = jnp.where(one, grad_params[KW + 1, 0], 0.0)

        def small_rows(gain_mix_row, gain_out_row):
            last = jnp.concatenate([gain_out_row, logs, biases])
            return jnp.concatenate(
                [
                    gain_mix_row,
                    grad_gain_ffn,
                    taps.reshape(KW, heads * qkv),
                    jnp.pad(last, (0, features - DV - 2 * heads)).reshape(1, features),
                    jnp.zeros((1, features), F32),
                ],
                axis=0,
            )

        if before is not None:
            summands, ffn_sums = lax.optimization_barrier((summands, ffn_sums))
        summands, project_sums = lax.optimization_barrier((summands, project_sums))
        sums = (ffn_sums, mix_sums, project_sums)
        source_shapes = (part_shape, shape((1, features), F32), shape((1, DV), F32))
        if before is not None:
            grad_input, grad_gain_mix, grad_gain_out, *up_halves, part, grad_gate, grad_up = local(
                source_ffn_grad,
                (*source_shapes, *halves, part_shape, active_shape, active_shape),
                (
                    flag,
                    gain_mix,
                    kept["source"],
                    *summands,
                    grad_stream,
                    w_back,
                    before["gate"],
                    before["up"],
                    w_hidden,
                ),
                6 * rows * features * hidden_width,
                "source_ffn_grad",
                choices[0],
            )
            before.update(up_low=grad_input, up_halves=up_halves, part=part)
            before.update(grad_gate=grad_gate, grad_up=grad_up)
            return grad_input, (*sums, small_rows(grad_gain_mix, grad_gain_out[0]))
        grad_input, grad_gain_mix, grad_gain_out = local(
            source_grad,
            source_shapes,
            (gain_mix, kept["source"], grad_stream, *summands),
            10 * rows * features,
            "source_grad",
        )
        return grad_input, (*sums, small_rows(grad_gain_mix, grad_gain_out[0])), earlier

    def settle(a_first, a_final):
        return (a_first, a_final), (swap_section(a_first), swap_section(a_final))

    def ordered(flag_now, mine, others):
        mine, others = mine.astype(F32), others.astype(F32)
        first = jnp.broadcast_to(flag_now[:, :1], mine.shape) > 0.5
        return jnp.where(first, mine, others), jnp.where(first, others, mine)

    def join_ffn(flag_now, *parts_now):
        whole = jnp.concatenate(ordered(flag_now(), *[p() for p in parts_now]), axis=1)
        yield whole[: 2 * hidden_width]
        yield whole[2 * hidden_width :]

    addends, kept_first = forward(0, (inputs_own,))
    (hidden, part), kept_final = forward(1, addends)
    first = kept_final["source"]
    grad_first, sums_final = backward(1, kept_final, before=kept_first)
    final_parts = sum_heads(after(part, grad_first))
    final = (hidden + add_up(final_parts)).astype(BF16)
    grad_inputs, sums_first, sums_final = backward(0, kept_first, sums_final)

    def join_project(flag_now, mix_mine, mix_others, mine, others):
        flag_now, mine, others = flag_now(), mine(), others()
        whole = jnp.concatenate(ordered(flag_now, mix_mine(), mix_others()), axis=1)
        yield whole[: heads * DV]
        gate_columns = whole[heads * DV :].T
        pieces, rates = [], [[], []]
        for h in range(heads):
            at = h * splits
            pair = [ordered(flag_now, mine[at + j], others[at + j]) for j in range(splits)]
            total = [sum((p[c] for p in pair[1:]), pair[0][c]) for c in range(2)]
            pieces.append(jnp.concatenate([t[:half, : 2 * DK] for t in total], axis=0))
            for p in pair:
                pieces.append(jnp.concatenate([t[:half, 2 * DK :] for t in p], axis=0))
            pieces.append(gate_columns[:, h * DV : (h + 1) * DV])
            found = [rates_of(t[half:], half) for t in total]
            for r in range(2):
                rates[r].append(jnp.concatenate([f[r] for f in found], axis=1))
        rates = jnp.concatenate(rates[0] + rates[1] + [jnp.zeros((16 - 2 * heads, slab), F32)], axis=0)
        wide_pieces = jnp.concatenate(pieces, axis=1)
        yield jnp.stack([wide_pieces[:, h * columns : (h + 1) * columns] for h in range(heads)], axis=1)
        yield rates

    small = jnp.where(
        core == 0,
        sums_first[3] + swap_section(sums_first[3]),
        sums_final[3] + swap_section(sums_final[3]),
    )
    joined = local(
        join_ffn,
        (shape((2 * hidden_width, slab), F32), shape((hidden_width, slab), F32)),
        (flag, *settle(sums_first[0], sums_final[0])),
        1000000,
        "join_ffn",
        own_first,
    )
    step, beside = 1, [joined]
    while step < parts:
        small = small + lax.ppermute(small, AXES, route(lambda s, z, h: (s, z ^ step, h)))
        if beside:
            small, joined = lax.optimization_barrier((small, beside.pop()))
        step *= 2
    grad_hidden_w, grad_back_w = joined
    grad_mix_w, grad_project_w, rate = local(
        join_project,
        (
            shape((heads * DV, slab), F32),
            shape((slab, heads, columns), F32),
            shape((16, slab), F32),
        ),
        (flag, *settle(sums_first[1], sums_final[1]), *settle(sums_first[2], sums_final[2])),
        1000000,
        "join_project",
        own_first,
    )

    grad_hidden_w = jnp.transpose(grad_hidden_w.reshape(2, hidden_width, slab), (2, 0, 1))
    grad_mix_w = grad_mix_w.reshape(heads, DV, slab)
    grad_rate_w = jnp.transpose(rate[: 2 * heads].reshape(2, heads, slab), (0, 2, 1))
    grad_taps = small[2 : KW + 2].reshape(KW, heads, qkv)
    logs = small[KW + 2]

    def both(first_rows, final_rows):
        return jnp.where(
            core == 0,
            jnp.stack([first_rows, swap_section(first_rows)]),
            jnp.stack([swap_section(final_rows), final_rows]),
        )

    block_out = both(first, final)
    input_grad = both(grad_inputs, grad_first)
    return (
        block_out[None],
        input_grad[None],
        small[None, :2],
        grad_project_w[None],
        grad_rate_w[None],
        logs[None, DV : DV + heads],
        logs[None, DV + heads : DV + 2 * heads],
        grad_taps[None],
        logs[None, :DV],
        grad_mix_w[None],
        grad_hidden_w[None],
        grad_back_w[None],
    )


def solution(mesh):
    placed = (
        P(None, "seq", None),
        P(None, "seq", None),
        P("section", None, None),
        P("section", None, "head", None),
        P("section", None, None, "head"),
        P("section", "head"),
        P("section", "head"),
        P("section", None, "head", None),
        P("section", None),
        P("section", "head", None, None),
        P("section", None, None, "head"),
        P("section", "head", None),
    )
    return jax.shard_map(
        body,
        mesh=mesh,
        in_specs=placed,
        out_specs=(
            P("section", None, "seq", None),
            P("section", None, "seq", None),
            P("section", None, None),
            P("section", "seq", "head", None),
            P("section", None, "seq", "head"),
            P("section", "head"),
            P("section", "head"),
            P("section", None, "head", None),
            P("section", None),
            P("section", "head", None, "seq"),
            P("section", "seq", None, "head"),
            P("section", "head", "seq"),
        ),
        check_vma=False,
    )
```

```python
import functools
import math

import jax
import jax.numpy as jnp
from jax import lax
from jax.experimental import pallas as pl
from jax.experimental.pallas import tpu as pltpu
from jax.sharding import PartitionSpec as P

DK = 128
DV = 256
KW = 4
CHUNK = 128
LANES = 128
EPS = 1e-06
HEAD_EPS = 0.01
AXES = ("section", "seq", "head")
F32 = jnp.float32
BF16 = jnp.bfloat16


def route(move):
    sections, seqs, heads = (lax.axis_size(axis) for axis in AXES)
    pairs = []
    for s in range(sections):
        for z in range(seqs):
            for h in range(heads):
                s2, z2, h2 = move(s, z, h)
                pairs.append(((s * seqs + z) * heads + h, (s2 * seqs + z2) * heads + h2))
    return pairs


def swap_section(value):
    return lax.ppermute(value, AXES, route(lambda s, z, h: (1 - s, z, h)))


def sum_heads(part):
    return [part] + [
        lax.ppermute(part, AXES, route(lambda s, z, h: (s, z, h ^ k)))
        for k in range(1, lax.axis_size("head"))
    ]


def add_up(parts):
    parts = [part.astype(F32) for part in parts]
    while len(parts) > 1:
        parts = [a + b for a, b in zip(parts[::2], parts[1::2])]
    return parts[0]


def after(value, *first):
    return lax.optimization_barrier((value,) + first)[0]


def exchange_seq(value):
    return lax.all_to_all(value, "seq", 0, 0, tiled=False)


NN = (((1,), (0,)), ((), ()))
NT = (((1,), (1,)), ((), ()))
TN = (((0,), (0,)), ((), ()))


def raw(a, b, dims, passes):
    a_hi, b_hi = a.astype(BF16), b.astype(BF16)
    out = lax.dot_general(a_hi, b_hi, dims, preferred_element_type=F32)
    if passes > 1:
        a_lo = (a - a_hi.astype(F32)).astype(BF16)
        b_lo = (b - b_hi.astype(F32)).astype(BF16)
        out = out + lax.dot_general(a_hi, b_lo, dims, preferred_element_type=F32)
        out = out + lax.dot_general(a_lo, b_hi, dims, preferred_element_type=F32)
    return out


@functools.partial(jax.custom_vjp, nondiff_argnums=(2,))
def nn(a, b, passes=1):
    return raw(a, b, NN, passes)


nn.defvjp(
    lambda a, b, p: (raw(a, b, NN, p), (a, b)),
    lambda p, kept, g: (raw(g, kept[1], NT, p), raw(kept[0], g, TN, p)),
)


@functools.partial(jax.custom_vjp, nondiff_argnums=(2,))
def nt(a, b, passes=1):
    return raw(a, b, NT, passes)


nt.defvjp(
    lambda a, b, p: (raw(a, b, NT, p), (a, b)),
    lambda p, kept, g: (raw(g, kept[1], NN, p), raw(g, kept[0], TN, p)),
)


@functools.partial(jax.custom_vjp, nondiff_argnums=(2,))
def tn(a, b, passes=1):
    return raw(a, b, TN, passes)


tn.defvjp(
    lambda a, b, p: (raw(a, b, TN, p), (a, b)),
    lambda p, kept, g: (raw(kept[1], g, NT, p), raw(kept[0], g, NN, p)),
)


def lower_ones():
    rows = lax.broadcasted_iota(jnp.int32, (CHUNK, CHUNK), 0)
    columns = lax.broadcasted_iota(jnp.int32, (CHUNK, CHUNK), 1)
    return jnp.where(rows >= columns, 1.0, 0.0)


def split3(v):
    hi = v.astype(BF16)
    rest = v - hi.astype(F32)
    mid = rest.astype(BF16)
    return hi, mid, (rest - mid.astype(F32)).astype(BF16)


@jax.custom_vjp
def running(v):
    ones = lower_ones().astype(BF16)
    return sum(lax.dot_general(ones, piece, NN, preferred_element_type=F32) for piece in split3(v))


def running_back(kept, g):
    ones = lower_ones().astype(BF16)
    return (sum(lax.dot_general(ones, piece, TN, preferred_element_type=F32) for piece in split3(g)),)


running.defvjp(lambda v: (running(v), None), running_back)


def inverse_value(lowers):
    rows = lax.broadcasted_iota(jnp.int32, (CHUNK, CHUNK), 0)
    columns = lax.broadcasted_iota(jnp.int32, (CHUNK, CHUNK), 1)
    results = [jnp.where(rows == columns, 1.0, 0.0)] * len(lowers)
    size = 1
    while size < CHUNK:
        joined = (rows // (2 * size) == columns // (2 * size)) & (rows // size != columns // size)
        between = [jnp.where(joined, lower, 0.0) for lower in lowers]
        if size == 1:
            results = [r - b for r, b in zip(results, between)]
        else:
            middle = [raw(b, r, NN, 3) for r, b in zip(results, between)]
            results = [r - raw(r, m, NN, 3) for r, m in zip(results, middle)]
        size *= 2
    return tuple(results)


@jax.custom_vjp
def inverse(lowers, values):
    return inverse_value(lowers) if values is None else values


def inverse_keep(lowers, values):
    values = inverse(lowers, values)
    return values, values


def inverse_back(values, grads):
    first = [raw(value, g, TN, 1) for value, g in zip(values, grads)]
    return tuple(-raw(f, value, NT, 1) for f, value in zip(first, values)), None


inverse.defvjp(inverse_keep, inverse_back)


def roll_rows(v, distance):
    return pltpu.roll(v, distance, 0)


@functools.partial(jax.custom_vjp, nondiff_argnums=(1,))
def shift_rows(v, distance):
    rows = lax.broadcasted_iota(jnp.int32, v.shape, 0)
    return jnp.where(rows >= distance, roll_rows(v, distance), 0.0)


def shift_back(distance, kept, g):
    rows = lax.broadcasted_iota(jnp.int32, g.shape, 0)
    return (jnp.where(rows < g.shape[0] - distance, roll_rows(g, g.shape[0] - distance), 0.0),)


shift_rows.defvjp(lambda v, d: (shift_rows(v, d), None), shift_back)


@jax.custom_vjp
def split_rows(v):
    return tuple(v[i : i + CHUNK] for i in range(0, v.shape[0], CHUNK))


split_rows.defvjp(lambda v: (split_rows(v), None), lambda kept, g: (jnp.concatenate(g, axis=0),))


@jax.custom_vjp
def low(v):
    return v.astype(BF16).astype(F32)


low.defvjp(lambda v: (low(v), None), lambda kept, g: (g,))


@jax.custom_vjp
def softplus(v):
    return jnp.maximum(v, 0.0) + jnp.log1p(jnp.exp(-jnp.abs(v)))


softplus.defvjp(lambda v: (softplus(v), v), lambda v, g: (g * jax.nn.sigmoid(v),))


def silu(v):
    return v * jax.nn.sigmoid(v)


def unit_norm(v):
    return v * lax.rsqrt(jnp.sum(v * v, axis=-1, keepdims=True) + EPS)


def convolve(rows_in, taps):
    total = taps[KW - 1] * rows_in
    for j in range(KW - 1):
        total = total + taps[j] * shift_rows(rows_in, KW - 1 - j)
    return total


def to_column(row):
    wide = jnp.broadcast_to(row, (CHUNK, CHUNK))
    rows = lax.broadcasted_iota(jnp.int32, wide.shape, 0)
    columns = lax.broadcasted_iota(jnp.int32, wide.shape, 1)
    return jnp.sum(jnp.where(rows == columns, wide, 0.0), axis=1, keepdims=True)


def recurrence(
    x_q, x_k, x_v, decay_raw, strength_raw, taps_q, taps_k, taps_v, decay_log, decay_bias, solves=None
):
    queries = low(unit_norm(silu(convolve(x_q, taps_q))) * DK**-0.5)
    keys = low(unit_norm(silu(convolve(x_k, taps_k))))
    values = low(silu(convolve(x_v, taps_v)))
    strength = [to_column(jax.nn.sigmoid(row)) for row in strength_raw]
    decay_rows = [-jnp.exp(decay_log) * softplus(row + decay_bias) for row in decay_raw]
    log_decay = [to_column(row) for row in decay_rows]
    rows = lax.broadcasted_iota(jnp.int32, (CHUNK, CHUNK), 0)
    columns = lax.broadcasted_iota(jnp.int32, (CHUNK, CHUNK), 1)
    queries, keys, values = (split_rows(a) for a in (queries, keys, values))
    chunks = range(len(keys))
    totals = [running(jnp.broadcast_to(ld, (CHUNK, CHUNK))) for ld in log_decay]
    wholes = [jnp.sum(row, axis=1, keepdims=True) for row in decay_rows]
    within = []
    for total in totals:
        spread = total - total.T
        within.append(
            jnp.where(rows >= columns, jnp.exp(jnp.where(rows >= columns, spread, 0.0)), 0.0)
        )
    grown = [jnp.exp(total) for total in totals]
    weighted = [strength[i] * keys[i] for i in chunks]
    lowers = tuple(
        strength[i] * nt(keys[i], keys[i]) * jnp.where(rows > columns, within[i], 0.0)
        for i in chunks
    )
    solve = inverse(lowers, solves)
    part_v = [nn(solve[i], strength[i] * values[i]) for i in chunks]
    part_k = [nn(solve[i], weighted[i] * grown[i]) for i in chunks]
    scores = [nt(queries[i], keys[i]) * within[i] for i in chunks]
    ending = [keys[i] * jnp.exp(wholes[i] - totals[i]) for i in chunks]
    seen = [queries[i] * grown[i] - nn(scores[i], part_k[i]) for i in chunks]
    own = [nn(scores[i], part_v[i]) for i in chunks]
    forget = [tn(ending[i], part_k[i]) for i in chunks]
    learn = [tn(ending[i], part_v[i]) for i in chunks]
    state = jnp.zeros((DK, x_v.shape[1]), F32)
    out = []
    for i in chunks:
        out.append(nn(seen[i], state) + own[i])
        state = jnp.exp(wholes[i]) * state + learn[i] - nn(forget[i], state)
    return jnp.concatenate(out, axis=0), solve


def with_rates(channels, decay_row, strength_row):
    rows = []
    for row in (decay_row, strength_row):
        hi = row.astype(BF16).astype(F32)
        rows += [hi, row - hi]
    rows = jnp.concatenate(rows + [jnp.zeros((12, row.shape[1]), F32)], axis=0)
    missing = channels.shape[1] - rows.shape[1]
    rows = jnp.concatenate([rows, jnp.zeros((16, missing), F32)], axis=1)
    return jnp.concatenate([channels, rows], axis=0).astype(BF16)


def rates_of(rows, count):
    rows = rows.astype(F32)
    return rows[0:1, :count] + rows[1:2, :count], rows[2:3, :count] + rows[3:4, :count]


def unpack(mixed, params, width):
    chunks = mixed.shape[0]
    x = mixed[:, :CHUNK].reshape(chunks * CHUNK, mixed.shape[2]).astype(F32)
    rates = [rates_of(mixed[i, CHUNK:], CHUNK) for i in range(chunks)]
    taps_q = [params[j : j + 1, :DK] for j in range(KW)]
    taps_k = [params[j : j + 1, DK : 2 * DK] for j in range(KW)]
    taps_v = [params[j : j + 1, 2 * DK : 2 * DK + width] for j in range(KW)]
    return (
        x[:, :DK],
        x[:, DK : 2 * DK],
        x[:, 2 * DK :],
        [r[0] for r in rates],
        [r[1] for r in rates],
        taps_q,
        taps_k,
        taps_v,
        params[KW : KW + 1, 0:1],
        params[KW + 1 : KW + 2, 0:1],
    )


def recur_forward(mixed, params, width):
    out, solve = recurrence(*unpack(mixed, params, width))
    return out.astype(BF16), jnp.concatenate(solve, axis=0).astype(BF16)


def recur_backward(mixed, params, solves, grad_out, width):
    solves = tuple(v.astype(F32) for v in split_rows(solves))
    unused, back = jax.vjp(
        lambda *a: recurrence(*a, solves=solves)[0], *unpack(mixed, params, width)
    )
    g_q, g_k, g_v, g_decay, g_strength, g_tq, g_tk, g_tv, g_log, g_bias = back(grad_out.astype(F32))
    wide = mixed.shape[2]
    channels = jnp.concatenate([g_q, g_k, g_v], axis=1)
    grad_mixed = jnp.stack(
        [with_rates(c, d, g) for c, d, g in zip(split_rows(channels), g_decay, g_strength)]
    )
    rows = [jnp.concatenate([g_tq[j], g_tk[j], g_tv[j]], axis=1) for j in range(KW)]
    rows.append(jnp.broadcast_to(g_log, (1, wide)))
    rows.append(jnp.broadcast_to(g_bias, (1, wide)))
    rows.append(jnp.zeros((2, wide), F32))
    return grad_mixed, jnp.concatenate(rows, axis=0)


def dot(a, b, dims=NN):
    return lax.dot_general(a, b, dims, preferred_element_type=F32)


def norm_scale(v, eps):
    return lax.rsqrt(jnp.mean(v * v, axis=-1, keepdims=True) + eps)


def norm_back(v, scale, gain, grad):
    gained = gain * grad
    mean = jnp.mean(gained * v, axis=-1, keepdims=True)
    grad_v = scale * gained - v * (scale * scale * scale) * mean
    return grad_v, jnp.sum(grad * v * scale, axis=0, keepdims=True)


def silu_grad(v):
    s = jax.nn.sigmoid(v)
    return s * (1.0 + v * (1.0 - s))


class Fetched:
    def __init__(self, slot, copies, step):
        self.slot, self.copies, self.step = slot, copies, step

    def wait(self, first, last):
        for i in range(first, last):
            if self.copies[i] is not None:
                self.copies[i].wait()
                self.copies[i] = None

    def __call__(self):
        self.wait(0, len(self.copies))
        return self.slot[...]

    def rows(self, low_row, high_row):
        self.wait(low_row // self.step, -(-high_row // self.step))
        return self.slot[low_row:high_row]


def pieces_of(array):
    large = math.prod(array.shape) * array.dtype.itemsize > 1000000
    return 4 if large and len(array.shape) == 2 and array.shape[0] % 64 == 0 else 1


def local(function, shapes, operands, flops, name, choice=None):
    pairs = [op if isinstance(op, (tuple, list)) else (op,) for op in operands]
    flat = [a for pair in pairs for a in pair]
    outs = len(shapes)
    chosen = any(len(pair) > 1 for pair in pairs)

    def kernel(*refs):
        refs = list(refs)
        flag = refs.pop(0) if chosen else None
        sources = [[refs.pop(0) for _ in pair] for pair in pairs]
        results = [refs.pop(0) for _ in shapes]
        slots = [refs.pop(0) for _ in pairs]
        stages = [refs.pop(0) for _ in shapes]
        in_sem, out_sem = refs
        fetched, used = [], 0
        for choices, slot in zip(sources, slots):
            number = pieces_of(slot)
            step = slot.shape[0] // number
            waits = []
            for i in range(number):
                cut = (lambda r: r) if number == 1 else (lambda r: r.at[pl.ds(i * step, step)])
                copies = [pltpu.make_async_copy(cut(c), cut(slot), in_sem.at[used]) for c in choices]
                used += 1
                if len(copies) == 1:
                    copies[0].start()
                else:
                    pl.when(flag[0] == 1)(copies[0].start)
                    pl.when(flag[0] != 1)(copies[1].start)
                waits.append(copies[0])
            fetched.append(Fetched(slot, waits, step))
        leaving = []
        for i, value in enumerate(function(*fetched)):
            stages[i][...] = value
            leaving.append(pltpu.make_async_copy(stages[i], results[i], out_sem.at[i]))
            leaving[-1].start()
        for one in fetched:
            one.wait(0, len(one.copies))
        for copy in leaving:
            copy.wait()

    moved = sum(math.prod(a.shape) * a.dtype.itemsize for a in ([p[0] for p in pairs] + list(shapes)))
    far = pl.BlockSpec(memory_space=pltpu.HBM)
    return pl.pallas_call(
        kernel,
        out_shape=tuple(shapes),
        in_specs=[pl.BlockSpec(memory_space=pltpu.SMEM)] * chosen + [far] * len(flat),
        out_specs=(far,) * outs,
        scratch_shapes=[pltpu.VMEM(p[0].shape, p[0].dtype) for p in pairs]
        + [pltpu.VMEM(a.shape, a.dtype) for a in shapes]
        + [pltpu.SemaphoreType.DMA((sum(pieces_of(p[0]) for p in pairs),)), pltpu.SemaphoreType.DMA((outs,))],
        compiler_params=pltpu.CompilerParams(vmem_limit_bytes=60 * 1024 * 1024),
        cost_estimate=pl.CostEstimate(flops=flops, bytes_accessed=moved, transcendentals=0),
        name=name,
    )(*([choice] * chosen), *flat)


def body(
    inputs,
    cotangent,
    gains,
    w_in,
    w_rates,
    a_log,
    dt_bias,
    conv_kernel,
    out_gain,
    w_out,
    w_ffn_in,
    w_down,
):
    core = lax.axis_index("section")
    place = lax.axis_index("seq")
    parts = lax.axis_size("seq")
    micro, rows, features = inputs.shape
    heads = w_in.shape[2]
    columns = w_in.shape[3]
    qkv = 2 * DK + DV
    hidden_width = w_ffn_in.shape[3]
    splits = parts // heads
    width = DV // splits
    wide = 2 * DK + width
    tall = rows + 16
    own_head = place // splits
    own_split = place % splits
    slab = features // parts
    half = slab // 2
    shape = jax.ShapeDtypeStruct

    def pair(own):
        return own, swap_section(own)

    own_first = (core == 0).astype(jnp.int32).reshape(1)
    choices = (own_first, 1 - own_first)
    w_project = pair(w_in[0].reshape(features, heads * columns))
    rate_rows = jnp.transpose(w_rates[0], (0, 2, 1)).reshape(2 * heads, features)
    w_rate = pair(jnp.pad(rate_rows, ((0, 16 - 2 * heads), (0, 0))))
    logs = jnp.concatenate([out_gain[0], a_log[0], dt_bias[0]])
    flats = pair(
        jnp.concatenate(
            [
                gains[0],
                conv_kernel[0].reshape(KW, heads * qkv),
                jnp.pad(logs, (0, features - DV - 2 * heads)).reshape(1, features),
                jnp.zeros((1, features), F32),
            ],
            axis=0,
        )
    )
    w_mix = pair(w_out[0].reshape(heads * DV, features))
    w_hidden = pair(jnp.transpose(w_ffn_in[0], (1, 2, 0)).reshape(2 * hidden_width, features))
    w_back = pair(w_down[0])
    inputs_own = jnp.where(core == 0, inputs[0], inputs[1])

    def small_params(index, held):
        flat = jnp.where(core == index, *held)
        logs = flat[KW + 2 : KW + 3]
        taps = flat[2 : KW + 2].reshape(KW, heads, qkv)
        taps = lax.dynamic_index_in_dim(taps, own_head, 1, keepdims=False)
        taps_v = lax.dynamic_slice_in_dim(taps, 2 * DK + own_split * width, width, 1)
        log = lax.dynamic_index_in_dim(logs[0, DV : DV + heads], own_head, 0, keepdims=False)
        bias = lax.dynamic_index_in_dim(
            logs[0, DV + heads : DV + 2 * heads], own_head, 0, keepdims=False
        )
        params = jnp.concatenate(
            [
                jnp.concatenate([taps[:, : 2 * DK], taps_v], axis=1),
                jnp.full((1, wide), log),
                jnp.full((1, wide), bias),
                jnp.zeros((2, wide), F32),
            ],
            axis=0,
        )
        return flat[0:1], flat[1:2], logs[:, :DV], params

    smalls = [(jnp.where(core == 0, flats[0][0:1], flats[1][0:1]),), None]

    flag = jnp.broadcast_to(jnp.where(core == 0, 1.0, 0.0).astype(F32), (1, LANES))

    def by_core(flag_now, value):
        first = jnp.broadcast_to(flag_now[:, :half], (value.shape[0], half)) > 0.5
        mine, others = [], []
        for p in range(parts):
            a = value[:, p * slab : p * slab + half].astype(F32)
            b = value[:, p * slab + half : (p + 1) * slab].astype(F32)
            mine.append(jnp.where(first, a, b))
            others.append(jnp.where(first, b, a))
        return [jnp.concatenate(v, axis=1).astype(BF16) for v in (mine, others)]

    def project_grad(flag_now, normed_all, grad_mixed):
        normed_all, grad_mixed = normed_all(), grad_mixed()
        channels = grad_mixed[:, :rows].reshape(parts * rows, wide)
        product = dot(normed_all, channels, TN)
        rates = jnp.concatenate([grad_mixed[p, rows:, :rows] for p in range(parts)], axis=1)
        rates = dot(rates, normed_all)
        decay, strength = rates[0:1] + rates[1:2], rates[2:3] + rates[3:4]
        mine, others = [], []
        for p in range(parts):
            cuts = []
            for c in range(2):
                at = p * slab + c * half
                cut = slice(at, at + half)
                cuts.append(with_rates(product[cut], decay[:, cut], strength[:, cut]).astype(F32))
            first = jnp.broadcast_to(flag_now()[:, :1], cuts[0].shape) > 0.5
            mine.append(jnp.where(first, cuts[0], cuts[1]).astype(BF16))
            others.append(jnp.where(first, cuts[1], cuts[0]).astype(BF16))
        yield jnp.stack(mine)
        yield jnp.stack(others)

    halves = (shape((rows, parts * half), BF16),) * 2

    def outs_of(received, h):
        return jnp.concatenate([received[h * splits + j] for j in range(splits)], axis=1).astype(F32)

    def front(flag_now, gain, w_rate_now, w_proj, *addends):
        source = addends[0]().astype(F32)
        if len(addends) > 1:
            source = source + add_up([a() for a in addends[1:]])
        source_low = source.astype(BF16)
        yield source_low
        source = source_low.astype(F32)
        normed = (source * norm_scale(source, EPS) * gain()).astype(BF16)
        yield normed
        yield from by_core(flag_now(), normed)
        rates = dot(w_rate_now(), normed, NT)
        quarter = features // 4
        whole = 0.0
        for i in range(4):
            at = i * quarter
            whole = whole + dot(normed[:, at : at + quarter], w_proj.rows(at, at + quarter))
        sent, gates = [], []
        for h in range(heads):
            projected = whole[:, h * columns : (h + 1) * columns]
            for j in range(splits):
                v_at = 2 * DK + j * width
                channels = [projected[:, : 2 * DK], projected[:, v_at : v_at + width]]
                sent.append(
                    with_rates(
                        jnp.concatenate(channels, axis=1),
                        rates[h : h + 1],
                        rates[heads + h : heads + h + 1],
                    )
                )
            gates.append(projected[:, qkv:])
        yield jnp.stack(sent)
        yield jnp.concatenate(gates, axis=1)

    def recur(params, mixed):
        yield from recur_forward(mixed(), params(), width)

    def mix(gain_out, gates, w_mix_now, received):
        gated = []
        received, gates = received(), gates()
        for h in range(heads):
            out = outs_of(received, h)
            gate = gates[:, h * DV : (h + 1) * DV]
            gated.append((out * norm_scale(out, HEAD_EPS) * gain_out() * silu(gate)).astype(BF16))
        gated = jnp.concatenate(gated, axis=1)
        yield dot(gated, w_mix_now()).astype(BF16)
        yield gated

    def ffn(flag_now, gain, source, one, two, three, four, w_hidden_now, w_back_now):
        hidden = source().astype(F32) + add_up([one(), two(), three(), four()])
        yield hidden
        hidden_norm = (hidden * norm_scale(hidden, EPS) * gain()).astype(BF16)
        yield from by_core(flag_now(), hidden_norm)
        gate = dot(hidden_norm, w_hidden_now.rows(0, hidden_width), NT)
        yield gate
        up = dot(hidden_norm, w_hidden_now.rows(hidden_width, 2 * hidden_width), NT)
        yield up
        active = (silu(gate) * up).astype(BF16)
        yield active
        yield dot(active, w_back_now()).astype(BF16)

    def forward(index, addends):
        gain_mix = smalls[index][0]
        source, normed, *normed_halves, sent, gates = local(
            front,
            (
                shape((rows, features), BF16),
                shape((rows, features), BF16),
                *halves,
                shape((parts, tall, wide), BF16),
                shape((rows, heads * DV), F32),
            ),
            (flag, gain_mix, w_rate, w_project, *addends),
            2 * rows * features * heads * columns,
            "front",
            choices[index],
        )
        mixed = exchange_seq(sent)
        if index == 0:
            held = lax.optimization_barrier((*flats, sent))[:2]
            smalls[:] = [small_params(0, held), small_params(1, held)]
        gain_mix, gain_ffn, gain_out, params = smalls[index]
        recurrent, solves = local(
            recur,
            (shape((parts * rows, width), BF16), shape((parts * rows, CHUNK), BF16)),
            (params, mixed),
            20 * 2 * parts * rows * DK * DK,
            "recur_forward",
        )
        received = exchange_seq(recurrent.reshape(parts, rows, width))
        part, gated = local(
            mix,
            (shape((rows, features), BF16), shape((rows, heads * DV), BF16)),
            (gain_out, gates, w_mix, received),
            2 * rows * features * heads * DV,
            "mix",
            choices[index],
        )
        summands = sum_heads(part)
        gate_shape = shape((rows, hidden_width), F32)
        active_shape = shape((rows, hidden_width), BF16)
        part_shape = shape((rows, features), BF16)
        extra = {}
        if index == 0:
            hidden, *hidden_halves, gate, up, active, part = local(
                ffn,
                (shape((rows, features), F32), *halves, gate_shape, gate_shape, active_shape, part_shape),
                (flag, gain_ffn, source, *summands, w_hidden, w_back),
                6 * rows * features * hidden_width,
                "ffn",
                choices[index],
            )
            extra = dict(gate=gate, up=up)
        else:
            up_low = jnp.where(core == 0, cotangent[0], cotangent[1])
            hidden, *both_halves, grad_gate, grad_up, part_grad, active, part = local(
                ffn_both,
                (
                    shape((rows, features), F32),
                    *halves,
                    *halves,
                    active_shape,
                    active_shape,
                    part_shape,
                    active_shape,
                    part_shape,
                ),
                (flag, gain_ffn, source, *summands, up_low, w_hidden, w_back),
                12 * rows * features * hidden_width,
                "ffn_both",
                choices[index],
            )
            hidden_halves = both_halves[:2]
            extra = dict(up_low=up_low, up_halves=both_halves[2:], part=part_grad)
            extra.update(grad_gate=grad_gate, grad_up=grad_up)
        kept = dict(
            source=source,
            normed_halves=normed_halves,
            mixed=mixed,
            solves=solves,
            received=received,
            gates=gates,
            gated=gated,
            hidden=hidden,
            hidden_halves=hidden_halves,
            active=active,
            **extra,
            normed_all=lax.all_gather(after(normed, gated), "seq", axis=0, tiled=True),
        )
        if index == 0:
            summands = sum_heads(part)
            summands, kept["normed_all"] = lax.optimization_barrier((summands, kept["normed_all"]))
            return (hidden, *summands), kept
        return (hidden, part), kept

    def ffn_grad(flag_now, up_low, w_back_now, gate, up, w_hidden_now):
        yield from by_core(flag_now(), up_low())
        grad_active = dot(up_low(), w_back_now(), NT)
        gate, up = gate(), up()
        grad_gate = (grad_active * up * silu_grad(gate)).astype(BF16)
        grad_up = (grad_active * silu(gate)).astype(BF16)
        part = dot(grad_gate, w_hidden_now.rows(0, hidden_width))
        part = part + dot(grad_up, w_hidden_now.rows(hidden_width, 2 * hidden_width))
        yield part.astype(BF16)
        yield grad_gate
        yield grad_up

    def ffn_both(flag_now, gain, source, one, two, three, four, up_low, w_hidden_now, w_back_now):
        hidden = source().astype(F32) + add_up([one(), two(), three(), four()])
        yield hidden
        hidden_norm = (hidden * norm_scale(hidden, EPS) * gain()).astype(BF16)
        yield from by_core(flag_now(), hidden_norm)
        yield from by_core(flag_now(), up_low())
        gate = dot(hidden_norm, w_hidden_now.rows(0, hidden_width), NT)
        up = dot(hidden_norm, w_hidden_now.rows(hidden_width, 2 * hidden_width), NT)
        grad_active = dot(up_low(), w_back_now(), NT)
        grad_gate = (grad_active * up * silu_grad(gate)).astype(BF16)
        yield grad_gate
        grad_up = (grad_active * silu(gate)).astype(BF16)
        yield grad_up
        part = dot(grad_gate, w_hidden_now.rows(0, hidden_width))
        part = part + dot(grad_up, w_hidden_now.rows(hidden_width, 2 * hidden_width))
        yield part.astype(BF16)
        active = (silu(gate) * up).astype(BF16)
        yield active
        yield dot(active, w_back_now()).astype(BF16)

    def source_ffn_grad(
        flag_now, gain, source_low, one, two, three, four, grad_stream, w_back_now, gate, up, w_hidden_now
    ):
        grad_input, *rest = source_grad(gain, source_low, grad_stream, one, two, three, four)
        yield grad_input
        yield from rest
        yield from ffn_grad(flag_now, lambda: grad_input, w_back_now, gate, up, w_hidden_now)

    def mix_grad(
        flag_now, gain, gain_out, hidden, upstream, one, two, three, four, w_mix_now, received, gates
    ):
        hidden = hidden()
        grad_hidden_norm = add_up([one(), two(), three(), four()]).astype(BF16).astype(F32)
        grad_hidden, grad_gain = norm_back(hidden, norm_scale(hidden, EPS), gain(), grad_hidden_norm)
        grad_stream = upstream().astype(F32) + grad_hidden
        yield grad_stream
        yield grad_gain
        yield from by_core(flag_now(), grad_stream)
        grad_gated = dot(grad_stream.astype(BF16), w_mix_now(), NT)
        received, gates = received(), gates()
        sent, grad_gates, grad_gain_out = [], [], 0.0
        for h in range(heads):
            out, gate_pre = outs_of(received, h), gates[:, h * DV : (h + 1) * DV]
            g = grad_gated[:, h * DV : (h + 1) * DV]
            scale = norm_scale(out, HEAD_EPS)
            grad_gates.append((g * out * scale * gain_out() * silu_grad(gate_pre)).astype(BF16))
            grad_out, grad_one = norm_back(out, scale, gain_out(), g * silu(gate_pre))
            grad_gain_out = grad_gain_out + grad_one
            for j in range(splits):
                sent.append(grad_out[:, j * width : (j + 1) * width].astype(BF16))
        yield jnp.stack(sent)
        yield jnp.concatenate(grad_gates, axis=1)
        yield grad_gain_out

    def recur_grad(params, mixed, solves, grad_out):
        yield from recur_backward(mixed(), params(), solves(), grad_out(), width)

    def front_grad(w_rate_now, grad_gates, grad_gain_out, returned, w_proj):
        grads = []
        grad_rates = [[], []]
        grad_gates, returned = grad_gates(), returned()
        for h in range(heads):
            mine = [returned[h * splits + j] for j in range(splits)]
            channels = [m[:rows].astype(F32) for m in mine]
            pieces = [sum((c[:, : 2 * DK] for c in channels[1:]), channels[0][:, : 2 * DK]).astype(BF16)]
            pieces += [m[:rows, 2 * DK :] for m in mine]
            pieces.append(grad_gates[:, h * DV : (h + 1) * DV])
            grads += pieces
            rates = [rates_of(m[rows:], rows) for m in mine]
            for r in range(2):
                grad_rates[r].append(sum((x[r] for x in rates[1:]), rates[0][r]))
        grad_rates = grad_rates[0] + grad_rates[1] + [jnp.zeros((16 - 2 * heads, rows), F32)]
        grad_rates = jnp.concatenate(grad_rates, axis=0).astype(BF16)
        part = dot(grad_rates, w_rate_now(), TN)
        grad = jnp.concatenate(grads, axis=1)
        quarter = features // 4
        cuts = [dot(grad, w_proj.rows(i * quarter, (i + 1) * quarter), NT) for i in range(4)]
        part = part + jnp.concatenate(cuts, axis=1)
        extra = jnp.concatenate([grad_gain_out(), jnp.zeros((1, features - DV), F32)], axis=1)
        extra = jnp.concatenate([extra, jnp.zeros((15, features), F32)], axis=0)
        yield jnp.concatenate([part, extra], axis=0).astype(BF16)

    def source_grad(gain, source_low, grad_stream, one, two, three, four):
        source = source_low().astype(F32)
        scale = norm_scale(source, EPS)
        summed = add_up([one(), two(), three(), four()])
        grad_normed = summed[:rows].astype(BF16).astype(F32)
        grad_source, grad_gain = norm_back(source, scale, gain(), grad_normed)
        yield (grad_stream() + grad_source).astype(BF16)
        yield grad_gain
        yield summed[rows : rows + 1, :DV]

    def weight_grads(groups, at=None):
        operands, counts, total = [], [], 0
        for lefts, (mine, others) in groups:
            operands += [mine, swap_section(others)]
            for left in lefts:
                operands += [left, swap_section(left)]
            counts.append(len(lefts))
            total += sum(left.shape[1] for left in lefts)

        def products(*values):
            values = list(values)
            out = []
            for count in counts:
                right, right_other = values.pop(0), values.pop(0)
                for _ in range(count):
                    left, left_other = values.pop(0), values.pop(0)
                    both = dot(left(), right(), TN) + dot(left_other(), right_other(), TN)
                    out.append(both.astype(BF16))
            whole = jnp.concatenate(out, axis=0)
            whole = jnp.stack([whole[:, p * half : (p + 1) * half] for p in range(parts)])
            for first, last in spans:
                yield whole[:, first:last]

        spans = [(0, total)] if at is None else [(0, at), (at, total)]
        return local(
            products,
            [shape((parts, last - first, half), BF16) for first, last in spans],
            operands,
            4 * rows * total * parts * half,
            "weight_grads",
        )

    def scatter_sum(whole):
        return lax.psum_scatter(whole, "seq", scatter_dimension=0, tiled=False)

    active_shape = shape((rows, hidden_width), BF16)
    part_shape = shape((rows, features), BF16)

    def backward(index, kept, earlier=None, before=None, block_out=None):
        gain_mix, gain_ffn, gain_out, params = smalls[index]
        up_low = kept["up_low"]
        summands = sum_heads(kept["part"])
        ffn_whole = weight_grads(
            [
                ([kept["grad_gate"], kept["grad_up"]], kept["hidden_halves"]),
                ([kept["active"]], kept["up_halves"]),
            ],
            None if before is None else 3 * hidden_width // 2 // 16 * 16,
        )
        summands, ffn_whole = lax.optimization_barrier((summands, ffn_whole))
        if earlier is None:
            summands, kept["normed_all"] = lax.optimization_barrier((summands, kept["normed_all"]))
        ffn_sums = scatter_sum(ffn_whole[0])
        grad_stream, grad_gain_ffn, *stream_halves, sent, grad_gates, grad_gain_out = local(
            mix_grad,
            (
                shape((rows, features), F32),
                shape((1, features), F32),
                *halves,
                shape((parts, rows, width), BF16),
                shape((rows, heads * DV), BF16),
                shape((1, DV), F32),
            ),
            (
                flag,
                gain_ffn,
                gain_out,
                kept["hidden"],
                up_low,
                *summands,
                w_mix,
                kept["received"],
                kept["gates"],
            ),
            2 * rows * features * heads * DV,
            "mix_grad",
            choices[index],
        )
        grad_all = exchange_seq(sent).reshape(parts * rows, width)
        (mix_whole,) = weight_grads(
            [([kept["gated"]], stream_halves), ([grad_gates], kept["normed_halves"])]
        )
        grad_all, mix_whole = lax.optimization_barrier((grad_all, mix_whole))
        if earlier is not None:
            grad_all, *tied = lax.optimization_barrier((grad_all, *earlier[:2]))
            earlier = tuple(tied) + earlier[2:]
            mix_sums = scatter_sum(mix_whole)
        grad_mixed, grad_params = local(
            recur_grad,
            (shape((parts, tall, wide), BF16), shape((KW + 4, wide), F32)),
            (params, kept["mixed"], kept["solves"], grad_all),
            40 * 2 * parts * rows * DK * DK,
            "recur_backward",
        )
        returned = exchange_seq(grad_mixed)

        def project_part(normed_all, grad_mixed):
            mine, others = local(
                project_grad,
                (shape((parts, half + 16, wide), BF16),) * 2,
                (flag, normed_all, grad_mixed),
                2 * parts * rows * features * wide,
                "project_grad",
            )
            return (mine.astype(F32) + swap_section(others).astype(F32)).astype(BF16)

        if before is None:
            normed_final, mixed_final = earlier[2]
            mine = jnp.concatenate(
                [
                    project_part(kept["normed_all"], grad_mixed),
                    project_part(normed_final, after(mixed_final, sent)),
                ],
                axis=1,
            )
            returned, block_out, mine = lax.optimization_barrier((returned, block_out, mine))
            project_sums = exchange_seq(mine)
        else:
            mix_sums = scatter_sum(after(mix_whole, returned))
            ffn_rest = scatter_sum(after(ffn_whole[1], returned))
        (part,) = local(
            front_grad,
            (shape((rows + 16, features), BF16),),
            (w_rate, grad_gates, grad_gain_out, returned, w_project),
            2 * rows * features * heads * columns,
            "front_grad",
            choices[index],
        )
        summands = sum_heads(part)
        taps = jnp.zeros((KW, heads, qkv), F32)
        taps = lax.dynamic_update_slice(taps, grad_params[:KW, None, : 2 * DK], (0, own_head, 0))
        taps = lax.dynamic_update_slice(
            taps,
            grad_params[:KW, None, 2 * DK :],
            (0, own_head, 2 * DK + own_split * width),
        )
        one = jnp.arange(heads) == own_head
        logs = jnp.where(one, grad_params[KW, 0], 0.0)
        biases = jnp.where(one, grad_params[KW + 1, 0], 0.0)

        def small_rows(gain_mix_row, gain_out_row):
            last = jnp.concatenate([gain_out_row, logs, biases])
            return jnp.concatenate(
                [
                    gain_mix_row,
                    grad_gain_ffn,
                    taps.reshape(KW, heads * qkv),
                    jnp.pad(last, (0, features - DV - 2 * heads)).reshape(1, features),
                    jnp.zeros((1, features), F32),
                ],
                axis=0,
            )

        if before is not None:
            summands, ffn_sums = lax.optimization_barrier((summands, ffn_sums))
            ffn_sums = jnp.concatenate([ffn_sums, ffn_rest], axis=0)
        if before is None:
            sums = (ffn_sums, mix_sums, project_sums)
        else:
            sums = (ffn_sums, mix_sums, (kept["normed_all"], grad_mixed))
        source_shapes = (part_shape, shape((1, features), F32), shape((1, DV), F32))
        if before is not None:
            grad_input, grad_gain_mix, grad_gain_out, *up_halves, part, grad_gate, grad_up = local(
                source_ffn_grad,
                (*source_shapes, *halves, part_shape, active_shape, active_shape),
                (
                    flag,
                    gain_mix,
                    kept["source"],
                    *summands,
                    grad_stream,
                    w_back,
                    before["gate"],
                    before["up"],
                    w_hidden,
                ),
                6 * rows * features * hidden_width,
                "source_ffn_grad",
                choices[0],
            )
            before.update(up_low=grad_input, up_halves=up_halves, part=part)
            before.update(grad_gate=grad_gate, grad_up=grad_up)
            return grad_input, (*sums, small_rows(grad_gain_mix, grad_gain_out[0]))
        grad_input, grad_gain_mix, grad_gain_out = local(
            source_grad,
            source_shapes,
            (gain_mix, kept["source"], grad_stream, *summands),
            10 * rows * features,
            "source_grad",
        )
        return grad_input, (*sums, small_rows(grad_gain_mix, grad_gain_out[0])), earlier, block_out

    def settle(a_first, a_final):
        return (a_first, a_final), (swap_section(a_first), swap_section(a_final))

    def ordered(flag_now, mine, others):
        mine, others = mine.astype(F32), others.astype(F32)
        first = jnp.broadcast_to(flag_now[:, :1], mine.shape) > 0.5
        return jnp.where(first, mine, others), jnp.where(first, others, mine)

    def join_ffn(flag_now, *parts_now):
        whole = jnp.concatenate(ordered(flag_now(), *[p() for p in parts_now]), axis=1)
        yield whole[: 2 * hidden_width]
        yield whole[2 * hidden_width :]

    def both(first_rows, final_rows):
        return jnp.where(
            core == 0,
            jnp.stack([first_rows, swap_section(first_rows)]),
            jnp.stack([swap_section(final_rows), final_rows]),
        )

    addends, kept_first = forward(0, (inputs_own,))
    (hidden, part), kept_final = forward(1, addends)
    first = kept_final["source"]
    grad_first, sums_final = backward(1, kept_final, before=kept_first)
    final_parts = sum_heads(after(part, grad_first))
    final = (hidden + add_up(final_parts)).astype(BF16)
    grad_inputs, sums_first, sums_final, block_out = backward(
        0, kept_first, sums_final, block_out=both(first, final)
    )

    def join_project(flag_now, mix_mine, mix_others, mine, others):
        flag_now, mine, others = flag_now(), mine(), others()
        cut = mine.shape[1] // 2
        chosen = jnp.broadcast_to(flag_now[:, :1], (parts, cut, wide)) > 0.5
        mine = jnp.where(chosen, mine[:, :cut].astype(F32), mine[:, cut:].astype(F32))
        others = jnp.where(chosen, others[:, :cut].astype(F32), others[:, cut:].astype(F32))
        whole = jnp.concatenate(ordered(flag_now, mix_mine(), mix_others()), axis=1)
        yield whole[: heads * DV]
        gate_columns = whole[heads * DV :].T
        pieces, rates = [], [[], []]
        for h in range(heads):
            at = h * splits
            pair = [ordered(flag_now, mine[at + j], others[at + j]) for j in range(splits)]
            total = [sum((p[c] for p in pair[1:]), pair[0][c]) for c in range(2)]
            pieces.append(jnp.concatenate([t[:half, : 2 * DK] for t in total], axis=0))
            for p in pair:
                pieces.append(jnp.concatenate([t[:half, 2 * DK :] for t in p], axis=0))
            pieces.append(gate_columns[:, h * DV : (h + 1) * DV])
            found = [rates_of(t[half:], half) for t in total]
            for r in range(2):
                rates[r].append(jnp.concatenate([f[r] for f in found], axis=1))
        rates = jnp.concatenate(rates[0] + rates[1] + [jnp.zeros((16 - 2 * heads, slab), F32)], axis=0)
        wide_pieces = jnp.concatenate(pieces, axis=1)
        yield jnp.stack([wide_pieces[:, h * columns : (h + 1) * columns] for h in range(heads)], axis=1)
        yield rates

    small = jnp.where(
        core == 0,
        sums_first[3] + swap_section(sums_first[3]),
        sums_final[3] + swap_section(sums_final[3]),
    )
    joined = local(
        join_ffn,
        (shape((2 * hidden_width, slab), F32), shape((hidden_width, slab), F32)),
        (flag, *settle(sums_first[0], sums_final[0])),
        1000000,
        "join_ffn",
        own_first,
    )
    small_parts = [small] + [
        lax.ppermute(small, AXES, route(lambda s, z, h: (s, z ^ k, h))) for k in range(1, parts)
    ]
    small_parts, joined = lax.optimization_barrier((small_parts, joined))
    small = add_up(small_parts)
    grad_hidden_w, grad_back_w = joined
    project_sums, mix_first, small_parts = lax.optimization_barrier(
        (sums_first[2], sums_first[1], small_parts)
    )
    grad_mix_w, grad_project_w, rate = local(
        join_project,
        (
            shape((heads * DV, slab), F32),
            shape((slab, heads, columns), F32),
            shape((16, slab), F32),
        ),
        (flag, *settle(mix_first, sums_final[1]), project_sums, swap_section(project_sums)),
        1000000,
        "join_project",
        own_first,
    )

    grad_hidden_w = jnp.transpose(grad_hidden_w.reshape(2, hidden_width, slab), (2, 0, 1))
    grad_mix_w = grad_mix_w.reshape(heads, DV, slab)
    grad_rate_w = jnp.transpose(rate[: 2 * heads].reshape(2, heads, slab), (0, 2, 1))
    grad_taps = small[2 : KW + 2].reshape(KW, heads, qkv)
    logs = small[KW + 2]

    input_grad = both(grad_inputs, grad_first)
    return (
        block_out[None],
        input_grad[None],
        small[None, :2],
        grad_project_w[None],
        grad_rate_w[None],
        logs[None, DV : DV + heads],
        logs[None, DV + heads : DV + 2 * heads],
        grad_taps[None],
        logs[None, :DV],
        grad_mix_w[None],
        grad_hidden_w[None],
        grad_back_w[None],
    )


def solution(mesh):
    placed = (
        P(None, "seq", None),
        P(None, "seq", None),
        P("section", None, None),
        P("section", None, "head", None),
        P("section", None, None, "head"),
        P("section", "head"),
        P("section", "head"),
        P("section", None, "head", None),
        P("section", None),
        P("section", "head", None, None),
        P("section", None, None, "head"),
        P("section", "head", None),
    )
    return jax.shard_map(
        body,
        mesh=mesh,
        in_specs=placed,
        out_specs=(
            P("section", None, "seq", None),
            P("section", None, "seq", None),
            P("section", None, None),
            P("section", "seq", "head", None),
            P("section", None, "seq", "head"),
            P("section", "head"),
            P("section", "head"),
            P("section", None, "head", None),
            P("section", None),
            P("section", "head", None, "seq"),
            P("section", "seq", None, "head"),
            P("section", "head", "seq"),
        ),
        check_vma=False,
    )
```
